32 devices in a mesh: shot: 4 (over y, x), depth: 2 (over core), inline: 4 (over z).
Axes of the slice: x: 2, y: 2, z: 4, core: 2. Of those that a mesh axis runs over, the one named last changes fastest.
Arguments:
- gradient: float32 [4, 32, 512, 512], P('shot', 'depth', 'inline'), may hold values from -8 to 8
- signs: int32 [4, 512], P('shot'), may hold values from 0 to 1
- model: float32 [32, 512, 512], P('depth', 'inline'), may hold values from 1.5 to 4.5
Outputs:
- updated: float32 [32, 512, 512], P('depth', 'inline')
The draws below stay inside these ranges and needn't reach their ends.
Inputs may be any that keep to these rules, and one draw needn't show every extreme that they name: `signs`: each bit s gives the sign 2 s - 1 of one crossline column of one group's partial.
All inputs are finite; a program needn't handle non-finite values.
Results may differ from the reference program's by a relative error of at most 0.00002.
Values sent between devices are 32-bit elements; how exact they have to be, the bound alone decides.
No kernel may reach another device: no remote copies, remote signals or barrier semaphores. Data moves between devices by JAX's collectives and lax.ppermute only.
A program may use at most 128 MiB of HBM per device.

```python
import jax
import jax.numpy as jnp
from jax import lax

ITERS = 3
NZ = 32
NX = 512
NY = 512
N_SHOT = 4


def with_ends(array, rng, least, top_value):
    dims = array.shape
    place = [jax.random.randint(jax.random.fold_in(rng, axis), (), 0, dims[axis]) for axis in range(len(dims))]
    array = array.at[tuple(place)].set(least)
    longest = dims.index(max(dims))
    place[longest] = (place[longest] + 1) % dims[longest]
    return array.at[tuple(place)].set(top_value)


def spiked(entries, rng, source, target, blocks, factor):
    def block_of(axis_at):
        return (jnp.arange(entries.shape[axis_at]) // (entries.shape[axis_at] // blocks)).reshape((-1,) + (1,) * (entries.ndim - 1 - axis_at))

    one_side = jax.random.permutation(rng, blocks)[block_of(target)]
    other_side = (block_of(target) + blocks // 2) % blocks
    return jnp.where((block_of(source) == one_side) | (block_of(source) == other_side), factor * entries, entries)


def level_of(rng, shape, pieces, low, top_value):
    def one(axis_at, parts):
        heights = jax.random.uniform(jax.random.fold_in(jax.random.fold_in(rng, 6), axis_at), (parts,), jnp.float32, low / len(pieces), top_value / len(pieces))
        return jnp.repeat(jnp.exp(heights), shape[axis_at] // parts).reshape((-1,) + (1,) * (len(shape) - axis_at - 1))

    loudness = one(*pieces[0])
    for cut in pieces[1:]:
        loudness = loudness * one(*cut)
    return loudness


def bell_draw_with(stream_key, extent, spread, most, split, heavy, held_as=jnp.bfloat16):
    entries = spread * jax.random.normal(stream_key, extent, jnp.float32)
    if split:
        entries = entries * level_of(stream_key, extent, split, -0.22, 0.18)
    return jnp.clip(spiked(entries, jax.random.fold_in(stream_key, 3), *heavy), -most, most).astype(held_as)


def setup_inputs(seed: int = 0) -> dict:
    streams_of = jax.random.split(jax.random.key(seed), 4)
    return {
        "gradient": bell_draw_with(streams_of[0], (N_SHOT, NZ, NX, NY), 1.0, 8.0, ((0, 4), (1, 2), (2, 4)), (0, 3, 4, 2.0), jnp.float32),
        "signs": with_ends(jax.random.randint(streams_of[1], (N_SHOT, NY), 0, 2), jax.random.fold_in(streams_of[1], 1), 0, 1).astype(jnp.int32),
        "model": jnp.clip(1.5 + 3.0 * jax.random.uniform(streams_of[2], (NZ, NX, NY), jnp.float32) ** level_of(streams_of[2], (NZ, NX, NY), ((0, 2), (1, 4)), -0.2, 0.2), 1.5, 4.5),
    }


step_tau = 0.28
step_sigma = 0.28
radius = 0.3
rate = 0.5

def forward_diff(field, axis):
    size = field.shape[axis]
    ahead = lax.slice_in_dim(field, 1, size, axis=axis) - lax.slice_in_dim(field, 0, size - 1, axis=axis)
    zero_shape = list(field.shape)
    zero_shape[axis] = 1
    return jnp.concatenate([ahead, jnp.zeros(zero_shape, jnp.float32)], axis=axis)

def backward_diff(field, axis):
    size = field.shape[axis]
    zero_shape = list(field.shape)
    zero_shape[axis] = 1
    before = jnp.concatenate([jnp.zeros(zero_shape, jnp.float32), lax.slice_in_dim(field, 0, size - 1, axis=axis)], axis=axis)
    return field - before

def reference(gradient, signs, model):
    decoded = jnp.zeros(model.shape, jnp.float32)
    for group in range(N_SHOT):
        factor = (2 * signs[group] - 1).astype(jnp.float32)
        decoded = decoded + gradient[group] * factor[None, None, :]
    target = model - rate * decoded
    primal = target
    extrapolated = target
    dual_z = jnp.zeros(model.shape, jnp.float32)
    dual_x = jnp.zeros(model.shape, jnp.float32)
    dual_y = jnp.zeros(model.shape, jnp.float32)
    for step in range(ITERS):
        qz = dual_z + step_sigma * forward_diff(extrapolated, 0)
        qx = dual_x + step_sigma * forward_diff(extrapolated, 1)
        qy = dual_y + step_sigma * forward_diff(extrapolated, 2)
        length = jnp.sqrt(qz * qz + qx * qx + qy * qy)
        scale = 1.0 / jnp.maximum(1.0, length / radius)
        dual_z, dual_x, dual_y = (qz * scale, qx * scale, qy * scale)
        diverge = backward_diff(dual_z, 0) + backward_diff(dual_x, 1) + backward_diff(dual_y, 2)
        fresh = (primal + step_tau * diverge + step_tau * target) / (1.0 + step_tau)
        extrapolated = 2.0 * fresh - primal
        primal = fresh
    return primal
```

```python
import functools

import jax
import jax.numpy as jnp
from jax import lax
from jax.experimental import pallas as pl
from jax.experimental.pallas import tpu as pltpu
from jax.sharding import PartitionSpec as P

ITERS = 3
HALO = 3
SIDE = 8
VMEM_LIMIT = 32 * 1024 * 1024

step_tau = 0.28
step_sigma = 0.28
radius = 0.3
rate = 0.5

keep_old = 1.0 / (1.0 + step_tau)
take_new = step_tau / (1.0 + step_tau)

PAIRS_X = [(0, 1), (1, 0), (2, 3), (3, 2)]
PAIRS_Y = [(0, 2), (2, 0), (1, 3), (3, 1)]


def swap_x(array):
    return lax.ppermute(array, "shot", PAIRS_X)


def swap_y(array):
    return lax.ppermute(array, "shot", PAIRS_Y)


def params():
    return pltpu.CompilerParams(vmem_limit_bytes=VMEM_LIMIT)


def tile_rows(rows):
    return slice(rows * SIDE, rows * SIDE + SIDE)


def prepare_kernel(place, sign_a, sign_b, grad_a, grad_b, out_a, out_b):
    out_a[0] = grad_a[0] * sign_a[...][None]
    out_b[0] = grad_b[0] * sign_b[...][None]


def prepare(place, sign, gradient, shares):
    _, planes, rows, cols = gradient.shape
    share, half, steps = (rows // shares, cols // 2, 2)
    part = planes // steps
    spec = pltpu.PrefetchScalarGridSpec(
        num_scalar_prefetch=1,
        grid=(2, steps),
        in_specs=[
            pl.BlockSpec((1, half), lambda i, z, place: (0, 0)),
            pl.BlockSpec((1, half), lambda i, z, place: (0, 1)),
            pl.BlockSpec((1, part, share, half), lambda i, z, place: (0, z, place[1 + i], 0)),
            pl.BlockSpec((1, part, share, half), lambda i, z, place: (0, z, place[3 - i], 1)),
        ],
        out_specs=[pl.BlockSpec((1, part, share, half), lambda i, z, place: (i, z, 0, 0))] * 2,
    )
    shape = jax.ShapeDtypeStruct((2, planes, share, half), jnp.float32)
    return pl.pallas_call(prepare_kernel, grid_spec=spec, out_shape=[shape] * 2, compiler_params=params())(
        place, sign, sign, gradient, gradient
    )


def relay_kernel(place, sign, grad, came, out):
    out[...] = grad[0] * sign[...][None] + came[0]


def relay(place, sign, gradient, came, which, side):
    _, planes, share, half = came.shape
    steps = 2
    part = planes // steps
    spec = pltpu.PrefetchScalarGridSpec(
        num_scalar_prefetch=1,
        grid=(steps,),
        in_specs=[
            pl.BlockSpec((1, half), lambda z, place: (0, side)),
            pl.BlockSpec((1, part, share, half), lambda z, place: (0, z, place[which], side)),
            pl.BlockSpec((1, part, share, half), lambda z, place: (1, z, 0, 0)),
        ],
        out_specs=pl.BlockSpec((part, share, half), lambda z, place: (z, 0, 0)),
    )
    return pl.pallas_call(
        relay_kernel,
        grid_spec=spec,
        out_shape=jax.ShapeDtypeStruct((planes, share, half), jnp.float32),
        compiler_params=params(),
    )(place, sign, gradient, came)


def settle_kernel(place, sign, grad, model, near_a, far_a, near_b, far_b, out):
    half = near_a.shape[3]
    own = grad[0] * sign[...][None]
    out[:, :, :half] = model[:, :, :half] - rate * (own[:, :, :half] + near_a[0] + far_a[...])
    out[:, :, half:] = model[:, :, half:] - rate * (own[:, :, half:] + near_b[0] + far_b[...])


def settle(place, sign, gradient, model, near_a, far_a, near_b, far_b):
    _, planes, share, half = near_a.shape
    cols, steps = (2 * half, 2)
    part = planes // steps
    near = pl.BlockSpec((1, part, share, half), lambda z, place: (0, z, 0, 0))
    far = pl.BlockSpec((part, share, half), lambda z, place: (z, 0, 0))
    spec = pltpu.PrefetchScalarGridSpec(
        num_scalar_prefetch=1,
        grid=(steps,),
        in_specs=[
            pl.BlockSpec((1, cols), lambda z, place: (0, 0)),
            pl.BlockSpec((1, part, share, cols), lambda z, place: (0, z, place[0], 0)),
            pl.BlockSpec((part, share, cols), lambda z, place: (z, place[0], 0)),
            near,
            far,
            near,
            far,
        ],
        out_specs=pl.BlockSpec((part, share, cols), lambda z, place: (z, 0, 0)),
    )
    return pl.pallas_call(
        settle_kernel,
        grid_spec=spec,
        out_shape=jax.ShapeDtypeStruct((planes, share, cols), jnp.float32),
        compiler_params=params(),
    )(place, sign, gradient, model, near_a, far_a, near_b, far_b)


def vary_kernel(total_z, total_x, where, mid, low, high, before, after, out_a, out_b, target, primal, ahead, dual):
    planes, rows, cols = target.shape
    share = mid.shape[1]
    half = cols // 2
    tiles = rows // SIDE
    shape = (SIDE, cols)
    own = planes - 2 * HALO

    def fill(p, source):
        target[p, 0:SIDE] = jnp.zeros(shape, jnp.float32)
        target[p, SIDE + share : rows] = jnp.zeros(shape, jnp.float32)
        target[p, SIDE : SIDE + share] = source
        target[p, SIDE - HALO : SIDE] = before[pl.ds(p * HALO, HALO), :]
        target[p, SIDE + share : SIDE + share + HALO] = after[pl.ds(p * HALO, HALO), :]

    for p in range(HALO):
        fill(p, low[p])
        fill(HALO + own + p, high[p])
    for p in range(own):
        fill(HALO + p, mid[p])

    row = lax.broadcasted_iota(jnp.int32, shape, 0)
    col = lax.broadcasted_iota(jnp.int32, shape, 1)
    first_row, last_row = (row == 0, row == SIDE - 1)
    coef_y = jnp.where(col < cols - 1, jnp.float32(step_sigma), jnp.float32(0))
    start_z, start_x = (where[0], where[1])

    def coef_x(t):
        place = start_x - SIDE + t * SIDE + row
        return jnp.where((place >= 0) & (place <= total_x - 2), jnp.float32(step_sigma), jnp.float32(0))

    edge_x = {t: coef_x(t) for t in (0, (SIDE + share) // SIDE - 1)}

    for step in range(ITERS):
        source = target if step == 0 else ahead
        old = target if step == 0 else primal

        def plane(p, carry):
            place = start_z - HALO + p
            coef_z = jnp.where((place >= 0) & (place <= total_z - 2), jnp.float32(step_sigma), jnp.float32(0))
            tile = [source[p, tile_rows(t)] for t in range(tiles)]
            turned = [pltpu.roll(v, SIDE - 1, 0) for v in tile]
            turned.append(turned[0])
            last_x = None
            for t in range(tiles):
                here = tile_rows(t)
                v = tile[t]
                step_z = coef_z * (source[p + 1, here] - v)
                step_x = edge_x.get(t, jnp.float32(step_sigma)) * (jnp.where(last_row, turned[t + 1], turned[t]) - v)
                step_y = coef_y * (pltpu.roll(v, cols - 1, 1) - v)
                if step > 0:
                    step_z = step_z + dual[0, p, here]
                    step_x = step_x + dual[1, p, here]
                    step_y = step_y + dual[2, p, here]
                square = step_z * step_z + step_x * step_x + step_y * step_y
                scale = jnp.minimum(jnp.float32(1), jnp.float32(radius) * lax.rsqrt(square))
                step_z, step_x, step_y = (step_z * scale, step_x * scale, step_y * scale)
                dual[0, p, here] = step_z
                if step < ITERS - 1:
                    dual[1, p, here] = step_x
                    dual[2, p, here] = step_y
                moved = pltpu.roll(step_x, 1, 0)
                if last_x is None:
                    last_x = moved
                diverge = (
                    (step_z - dual[0, jnp.maximum(p - 1, 0), here])
                    + (step_x - jnp.where(first_row, last_x, moved))
                    + (step_y - pltpu.roll(step_y, 1, 1))
                )
                last_x = moved
                before_it = old[p, here]
                fresh = jnp.float32(keep_old) * before_it + jnp.float32(take_new) * (diverge + target[p, here])
                if step < ITERS - 1:
                    primal[p, here] = fresh
                    ahead[p, here] = 2.0 * fresh - before_it
                elif 1 <= t < tiles - 1:
                    spot = jnp.maximum(p - HALO, 0)
                    there = tile_rows(t - 1)
                    out_a[spot, there] = fresh[:, :half]
                    out_b[spot, there] = fresh[:, half:]
            return carry

        lax.fori_loop(step, planes - 1 - step, plane, 0)


def vary(where, mid, low, high, before, after, total_z, total_x):
    own, share, cols = mid.shape
    planes, rows = (own + 2 * HALO, share + 2 * SIDE)
    whole = pl.BlockSpec(memory_space=pltpu.VMEM)
    shape = jax.ShapeDtypeStruct((own, share, cols // 2), jnp.float32)
    field = pltpu.VMEM((planes, rows, cols), jnp.float32)
    return pl.pallas_call(
        functools.partial(vary_kernel, total_z, total_x),
        in_specs=[pl.BlockSpec(memory_space=pltpu.SMEM)] + [whole] * 5,
        out_specs=[whole] * 2,
        out_shape=[shape] * 2,
        scratch_shapes=[field, field, field, pltpu.VMEM((3, planes, rows, cols), jnp.float32)],
        compiler_params=params(),
    )(where, mid, low, high, before, after)


def gather_kernel(place, own_a, own_b, x_a, x_b, y_a, y_b, far_a, far_b, out, sems):
    share, half = own_a.shape[1:]
    copies = []
    for which, (left, right) in enumerate(((own_a, own_b), (x_a, x_b), (far_a, far_b), (y_a, y_b))):
        rows = pl.ds(pl.multiple_of(place[which] * share, share), share)
        copies.append(pltpu.make_async_copy(left, out.at[:, rows, pl.ds(0, half)], sems.at[2 * which]))
        copies.append(pltpu.make_async_copy(right, out.at[:, rows, pl.ds(half, half)], sems.at[2 * which + 1]))
    for copy in copies:
        copy.start()
    for copy in copies:
        copy.wait()


def gather(place, shares, *pieces):
    planes, share, half = pieces[0].shape
    anywhere = pl.BlockSpec(memory_space=pl.ANY)
    return pl.pallas_call(
        gather_kernel,
        in_specs=[pl.BlockSpec(memory_space=pltpu.SMEM)] + [anywhere] * 8,
        out_specs=anywhere,
        out_shape=jax.ShapeDtypeStruct((planes, shares * share, 2 * half), jnp.float32),
        scratch_shapes=[pltpu.SemaphoreType.DMA((8,))],
        compiler_params=params(),
    )(place, *pieces)


def gray(place):
    return place ^ (place >> 1)


def body(gradient, signs, model):
    shares, lines, layers = (lax.axis_size(name) for name in ("shot", "inline", "depth"))
    planes, rows, cols = model.shape
    share = rows // shares
    total_z, total_x = (planes * layers, rows * lines)
    shot = lax.axis_index("shot")
    at = gray(shot)
    place = jnp.stack([at, at ^ 1, at ^ 2, at ^ 3]).astype(jnp.int32)
    start_z = lax.axis_index("depth") * planes
    start_x = lax.axis_index("inline") * rows + at * share
    where = jnp.stack([start_z, start_x]).astype(jnp.int32)
    sign = (2 * signs - 1).astype(jnp.float32)

    order = [gray(spot) * lines + line for line in range(lines) for spot in range(shares)]
    ahead_x = list(zip(order[:-1], order[1:]))
    back_x = [(j, i) for i, j in ahead_x]
    ahead_z = [(i, i + 1) for i in range(layers - 1)]
    back_z = [(j, i) for i, j in ahead_z]

    send_a, send_b = prepare(place, sign, gradient, shares)
    near_a, near_b = (swap_x(send_a), swap_y(send_b))
    far_a = swap_y(relay(place, sign, gradient, near_a, 3, 0))
    far_b = swap_x(relay(place, sign, gradient, near_b, 1, 1))
    target = settle(place, sign, gradient, model, near_a, far_a, near_b, far_b)

    low = lax.ppermute(target[planes - HALO :], "depth", ahead_z)
    high = lax.ppermute(target[:HALO], "depth", back_z)
    tops = jnp.concatenate([part[:, share - HALO :].reshape(-1, cols) for part in (low, target, high)], axis=0)
    feet = jnp.concatenate([part[:, :HALO].reshape(-1, cols) for part in (low, target, high)], axis=0)
    before = lax.ppermute(tops, ("shot", "inline"), ahead_x)
    after = lax.ppermute(feet, ("shot", "inline"), back_x)
    own_a, own_b = vary(where, target, low, high, before, after, total_z, total_x)

    y_a, x_b = (swap_y(own_a), swap_x(own_b))
    y_b, x_a = (swap_y(own_b), swap_x(own_a))
    far_a, far_b = (swap_x(y_a), swap_y(x_b))
    return gather(place, shares, own_a, own_b, x_a, x_b, y_a, y_b, far_a, far_b)


def solution(mesh):
    placed = (P("shot", "depth", "inline", None), P("shot", None), P("depth", "inline", None))
    return jax.shard_map(
        body, mesh=mesh, in_specs=placed, out_specs=P("depth", "inline", None), check_vma=False
    )
```

```python
import functools

import jax
import jax.numpy as jnp
from jax import lax
from jax.experimental import pallas as pl
from jax.experimental.pallas import tpu as pltpu
from jax.sharding import PartitionSpec as P

ITERS = 3
HALO = 3
SIDE = 8
VMEM_LIMIT = 16 * 1024 * 1024

step_tau = 0.28
step_sigma = 0.28
radius = 0.3
rate = 0.5

keep_old = 1.0 / (1.0 + step_tau)
take_new = step_tau / (1.0 + step_tau)

PAIRS_X = [(0, 1), (1, 0), (2, 3), (3, 2)]
PAIRS_Y = [(0, 2), (2, 0), (1, 3), (3, 1)]
PAIRS_FAR = [(0, 3), (3, 0), (1, 2), (2, 1)]


def swap_x(array):
    return lax.ppermute(array, "shot", PAIRS_X)


def swap_y(array):
    return lax.ppermute(array, "shot", PAIRS_Y)


def swap_far(array):
    return lax.ppermute(array, "shot", PAIRS_FAR)


def params():
    return pltpu.CompilerParams(vmem_limit_bytes=VMEM_LIMIT)


COST = pl.CostEstimate(flops=1, bytes_accessed=1, transcendentals=0)
HUGE = pl.CostEstimate(flops=1, bytes_accessed=1_000_000_000, transcendentals=0)
LONG = pl.CostEstimate(flops=1, bytes_accessed=100_000_000, transcendentals=0)


def tile_rows(rows):
    return slice(rows * SIDE, rows * SIDE + SIDE)


WHOLE = pl.BlockSpec(memory_space=pltpu.VMEM)
SCALARS = pl.BlockSpec(memory_space=pltpu.SMEM)
ANYWHERE = pl.BlockSpec(memory_space=pl.ANY)
FLIP, START_Z, START_X = (4, 5, 6)


def turn(flip, offset, count, total):
    return jnp.where(flip == 1, total - offset - count, offset)


def factor(signs):
    return (2 * signs[...] - 1).astype(jnp.float32)


def share_rows(spot, which, share):
    return pl.ds(pl.multiple_of(spot[which] * share, share), share)


def chunk_planes(spot, chunk, planes):
    offset, count = chunk
    return pl.ds(turn(spot[FLIP], offset, count, planes), count)


def fetch(source, spot, chunk, which, side, into, sem):
    planes, share, width = (source.shape[-3], into.shape[-2], into.shape[-1])
    place = (chunk_planes(spot, chunk, planes), share_rows(spot, which, share), pl.ds(side, width))
    if len(source.shape) == 4:
        place = (0,) + place
    copy = pltpu.make_async_copy(source.at[place], into, sem)
    copy.start()
    return copy


def prepare_kernel(chunk, after, spot, signs, gradient, *rest):
    out_a, out_b, held, held_signs, sems = rest[after:]
    half = out_a.shape[3]
    copy_signs = pltpu.make_async_copy(signs, held_signs, sems.at[4])
    copy_signs.start()
    todo = [(out_a, i, which, 0) for i, which in enumerate((1, 2))]
    todo += [(out_b, i, which, half) for i, which in enumerate((3, 2))]
    copies = [fetch(gradient, spot, chunk, which, side, held.at[n], sems.at[n]) for n, (_, _, which, side) in enumerate(todo)]
    copy_signs.wait()
    sign = factor(held_signs)[None]
    for n, (out, i, _, side) in enumerate(todo):
        copies[n].wait()
        out[i] = held[n] * sign[:, :, side : side + half]


def prepare(chunk, spot, signs, gradient, shares, after=()):
    rows, cols = gradient.shape[2:]
    shape = (2, chunk[1], rows // shares, cols // 2)
    return pl.pallas_call(
        functools.partial(prepare_kernel, chunk, len(after)),
        in_specs=[SCALARS] + [ANYWHERE] * (2 + len(after)),
        out_specs=[WHOLE] * 2,
        out_shape=[jax.ShapeDtypeStruct(shape, jnp.float32)] * 2,
        scratch_shapes=[
            pltpu.VMEM((4,) + shape[1:], jnp.float32),
            pltpu.VMEM(signs.shape, jnp.int32),
            pltpu.SemaphoreType.DMA((5,)),
        ],
        compiler_params=params(),
        cost_estimate=COST,
    )(spot, signs, gradient, *after)


def hold_kernel(chunks, after, spot, signs, gradient, model, *rest):
    fore_a, fore_b, base, held_a, held_b, held, held_signs, sems = rest[after:]
    half = fore_a.shape[2]
    copy_signs = pltpu.make_async_copy(signs, held_signs, sems.at[4 * len(chunks)])
    copy_signs.start()
    todo = []
    for chunk in chunks:
        here = pl.ds(*chunk)
        parts = ((gradient, 3, 0, held_a), (gradient, 1, half, held_b), (gradient, 0, 0, held.at[0]), (model, 0, 0, held.at[1]))
        copies = [
            fetch(source, spot, chunk, which, side, into.at[here], sems.at[len(todo) * 4 + n])
            for n, (source, which, side, into) in enumerate(parts)
        ]
        todo.append((copies, slice(chunk[0], chunk[0] + chunk[1])))
    copy_signs.wait()
    sign = factor(held_signs)[None]
    for copies, here in todo:
        for copy in copies:
            copy.wait()
        fore_a[here] = held_a[here] * sign[:, :, :half]
        fore_b[here] = held_b[here] * sign[:, :, half:]
        base[here] = held[1, here] - rate * (held[0, here] * sign)


def hold(chunks, spot, signs, gradient, model, shares, after=()):
    planes, rows, cols = model.shape
    whole = (planes, rows // shares, cols)
    part = (planes, rows // shares, cols // 2)
    return pl.pallas_call(
        functools.partial(hold_kernel, chunks, len(after)),
        in_specs=[SCALARS] + [ANYWHERE] * (3 + len(after)),
        out_specs=[WHOLE] * 3,
        out_shape=[pltpu.VMEM(shape, jnp.float32) for shape in (part, part, whole)],
        scratch_shapes=[
            pltpu.VMEM(part, jnp.float32),
            pltpu.VMEM(part, jnp.float32),
            pltpu.VMEM((2,) + whole, jnp.float32),
            pltpu.VMEM(signs.shape, jnp.int32),
            pltpu.SemaphoreType.DMA((4 * len(chunks) + 1,)),
        ],
        compiler_params=params(),
        cost_estimate=COST,
    )(spot, signs, gradient, model, *after)


def relay_kernel(chunk, ready, after, fore_a, fore_b, near_a, near_b, *rest):
    out_a, out_b = rest[ready + after :]
    at = 0
    if ready:
        at = rest[0].shape[0]
        out_a[:at] = rest[0][...]
        out_b[:at] = rest[1][...]
    here = slice(chunk[0], chunk[0] + chunk[1])
    out_a[at:] = fore_a[here] + near_a[1]
    out_b[at:] = fore_b[here] + near_b[1]


def relay(chunk, fores, near, ready=(), after=()):
    count = chunk[1] + sum(part.shape[0] for part in ready[:1])
    return pl.pallas_call(
        functools.partial(relay_kernel, chunk, len(ready), len(after)),
        in_specs=[WHOLE] * (4 + len(ready)) + [ANYWHERE] * len(after),
        out_specs=[WHOLE] * 2,
        out_shape=[jax.ShapeDtypeStruct((count,) + near[0].shape[2:], jnp.float32)] * 2,
        compiler_params=params(),
        cost_estimate=COST,
    )(*fores, *near, *ready, *after)


def settle_kernel(chunks, after, base, *refs):
    nears, (far_a, far_b) = (refs[: 2 * len(chunks)], refs[2 * len(chunks) : 2 * len(chunks) + 2])
    out = refs[-1]
    half = far_a.shape[2]
    at = 0
    for k, (start, count) in enumerate(chunks):
        here = slice(at, at + count)
        for side, near, far in ((slice(0, half), nears[2 * k], far_a), (slice(half, 2 * half), nears[2 * k + 1], far_b)):
            out[here, :, side] = base[start : start + count, :, side] - rate * (near[0] + far[here])
        at += count


def settle(chunks, base, nears, fars, after=()):
    count, share, half = fars[0].shape
    return pl.pallas_call(
        functools.partial(settle_kernel, chunks, len(after)),
        in_specs=[WHOLE] * (3 + len(nears)) + [ANYWHERE] * len(after),
        out_specs=WHOLE,
        out_shape=jax.ShapeDtypeStruct((count, share, 2 * half), jnp.float32),
        compiler_params=params(),
        cost_estimate=COST,
    )(base, *nears, *fars, *after)


def pack_kernel(count, *refs):
    parts, (tops, feet) = (refs[:count], refs[count:])
    at = 0
    for part in parts:
        for p in range(part.shape[0]):
            tops[at] = part[p, part.shape[1] - HALO :]
            feet[at] = part[p, :HALO]
            at += 1


def pack(parts):
    shape = (sum(part.shape[0] for part in parts), HALO, parts[0].shape[2])
    return pl.pallas_call(
        functools.partial(pack_kernel, len(parts)),
        in_specs=[WHOLE] * len(parts),
        out_specs=[WHOLE] * 2,
        out_shape=[jax.ShapeDtypeStruct(shape, jnp.float32)] * 2,
        compiler_params=params(),
        cost_estimate=COST,
    )(*parts)


def vary_kernel(span, pieces, sizes, counts, after, spot, *refs):
    fields, befores, afters = (refs[: counts[0]], refs[counts[0] : counts[0] + counts[1]], refs[counts[0] + counts[1] : counts[0] + 2 * counts[1]])
    out, target, primal, ahead, dual = refs[counts[0] + 2 * counts[1] + after :]
    planes, rows, cols = target.shape
    depth_planes, total_z, total_x = sizes
    share = rows - SIDE
    half = cols // 2
    tiles = share // SIDE
    shape = (SIDE, cols)
    flip = spot[FLIP]

    for field, held, offset, count, side, line, there, base in pieces:
        goes = turn(flip, there, count, planes)
        if field is None:
            for i in range(count):
                target[goes + i] = jnp.zeros((rows, cols), jnp.float32)
            continue
        comes = turn(flip, offset, count, held)
        for i in range(count):
            target[goes + i, :share] = fields[field][base + comes + i]
            target[goes + i, share:rows] = jnp.zeros(shape, jnp.float32)
            target[goes + i, share : share + HALO] = afters[side][line + comes + i]
            target[goes + i, rows - HALO : rows] = befores[side][line + comes + i]

    row = lax.broadcasted_iota(jnp.int32, shape, 0)
    col = lax.broadcasted_iota(jnp.int32, shape, 1)
    first_row, last_row = (row == 0, row == SIDE - 1)
    coef_y = jnp.where(col < cols - 1, jnp.float32(step_sigma), jnp.float32(0))
    start_x = spot[START_X]
    start_z = spot[START_Z] + turn(flip, span[0] - HALO, planes, depth_planes)

    def coef_x(place):
        return jnp.where((place >= 0) & (place <= total_x - 2), jnp.float32(step_sigma), jnp.float32(0))

    edge_x = {
        tiles - 1: coef_x(start_x + share - SIDE + row),
        tiles: coef_x(start_x + jnp.where(row < SIDE // 2, share + row, row - SIDE)),
    }

    for step in range(ITERS):
        source = target if step == 0 else ahead
        old = target if step == 0 else primal

        def plane(p, carry):
            place = start_z + p
            coef_z = jnp.where((place >= 0) & (place <= total_z - 2), jnp.float32(step_sigma), jnp.float32(0))
            tile = [source[p, tile_rows(t)] for t in range(tiles + 1)]
            turned = [pltpu.roll(v, SIDE - 1, 0) for v in tile]

            def steps_of(t):
                here = tile_rows(t)
                v = tile[t]
                beyond = turned[(t + 1) % (tiles + 1)]
                step_z = coef_z * (source[p + 1, here] - v)
                step_x = edge_x.get(t, jnp.float32(step_sigma)) * (jnp.where(last_row, beyond, turned[t]) - v)
                step_y = coef_y * (pltpu.roll(v, cols - 1, 1) - v)
                if step > 0:
                    step_z = step_z + dual[0, p, here]
                    step_x = step_x + dual[1, p, here]
                    step_y = step_y + dual[2, p, here]
                square = step_z * step_z + step_x * step_x + step_y * step_y
                scale = jnp.minimum(jnp.float32(1), jnp.float32(radius) * lax.rsqrt(square))
                step_z, step_x, step_y = (step_z * scale, step_x * scale, step_y * scale)
                dual[0, p, here] = step_z
                if step < ITERS - 1:
                    dual[1, p, here] = step_x
                    dual[2, p, here] = step_y
                return step_z, step_x, step_y, pltpu.roll(step_x, 1, 0)

            def renew(t, steps, last_x):
                here = tile_rows(t)
                step_z, step_x, step_y, moved = steps
                diverge = (
                    (step_z - dual[0, jnp.maximum(p - 1, 0), here])
                    + (step_x - jnp.where(first_row, last_x, moved))
                    + (step_y - pltpu.roll(step_y, 1, 1))
                )
                before_it = old[p, here]
                fresh = jnp.float32(keep_old) * before_it + jnp.float32(take_new) * (diverge + target[p, here])
                if step < ITERS - 1:
                    primal[p, here] = fresh
                    ahead[p, here] = 2.0 * fresh - before_it
                else:
                    place_out = jnp.maximum(p - HALO, 0)
                    out[0, place_out, here] = fresh[:, :half]
                    out[1, place_out, here] = fresh[:, half:]

            edge_steps = steps_of(tiles)
            last_x = edge_steps[3]
            for t in range(tiles):
                steps = steps_of(t)
                renew(t, steps, last_x)
                last_x = steps[3]
            if step < ITERS - 1:
                renew(tiles, edge_steps, last_x)
            return carry

        lax.fori_loop(step, planes - 1 - step, plane, 0)


def vary(span, pieces, sizes, spot, fields, befores, afters, after=()):
    _, share, cols = fields[0].shape
    planes, rows = (span[1] - span[0] + 2 * HALO, share + SIDE)
    field = pltpu.VMEM((planes, rows, cols), jnp.float32)
    counts = (len(fields), len(befores))
    return pl.pallas_call(
        functools.partial(vary_kernel, span, pieces, sizes, counts, len(after)),
        in_specs=[SCALARS] + [WHOLE] * (counts[0] + 2 * counts[1]) + [ANYWHERE] * len(after),
        out_specs=WHOLE,
        out_shape=jax.ShapeDtypeStruct((2, span[1] - span[0], share, cols // 2), jnp.float32),
        scratch_shapes=[field, field, field, pltpu.VMEM((3, planes, rows, cols), jnp.float32)],
        compiler_params=params(),
        cost_estimate=LONG,
    )(spot, *fields, *befores, *afters, *after)


def gather_kernel(span, parts, spot, *refs):
    out, sems = refs[-2:]
    layers = chunk_planes(spot, (span[0], span[1] - span[0]), out.shape[0])
    copies = []
    for ref, (which, sides) in zip(refs, parts):
        share, half = ref.shape[-2:]
        for n, side in enumerate(sides):
            there = out.at[layers, share_rows(spot, which, share), pl.ds(side * half, half)]
            source = ref.at[n] if len(ref.shape) == 4 else ref
            copies.append(pltpu.make_async_copy(source, there, sems.at[len(copies)]))
    for copy in copies:
        copy.start()
    for copy in copies:
        copy.wait()


def gather(span, spot, out_shape, pieces, so_far=None, cost=COST):
    before = [] if so_far is None else [so_far]
    arrays, parts = zip(*((array, (which, sides)) for array, which, sides in pieces))
    return pl.pallas_call(
        functools.partial(gather_kernel, span, parts),
        in_specs=[SCALARS] + [ANYWHERE] * (len(arrays) + len(before)),
        out_specs=pl.BlockSpec(memory_space=pltpu.HBM),
        out_shape=jax.ShapeDtypeStruct(out_shape, jnp.float32),
        input_output_aliases={1 + len(arrays): 0} if before else {},
        scratch_shapes=[pltpu.SemaphoreType.DMA((8,))],
        compiler_params=params(),
        cost_estimate=cost,
    )(spot, *arrays, *before)


def idle_kernel(*refs):
    pass


def idle(arrays, after):
    return pl.pallas_call(
        idle_kernel,
        in_specs=[ANYWHERE] * (len(arrays) + len(after)),
        out_specs=[ANYWHERE] * len(arrays),
        out_shape=[jax.ShapeDtypeStruct(array.shape, array.dtype) for array in arrays],
        input_output_aliases={i: i for i in range(len(arrays))},
        cost_estimate=COST,
    )(*arrays, *after)


def gray(place):
    return place ^ (place >> 1)


def spread(own):
    from_x, from_y = (swap_x(own), swap_y(own))
    far_a, far_b = (swap_x(from_y[0]), swap_y(from_x[1]))
    return ((own, 0, (0, 1)), (from_x, 1, (0, 1)), (far_a, 2, (0,)), (far_b, 2, (1,)), (from_y, 3, (0, 1)))


def spread_halves(own):
    y_a, x_b = (swap_y(own[0]), swap_x(own[1]))
    x_a, y_b = (swap_x(own[0]), swap_y(own[1]))
    far_a, far_b = (swap_x(y_a), swap_y(x_b))
    return (
        (own, 0, (0, 1)), (x_a, 1, (0,)), (x_b, 1, (1,)), (far_a, 2, (0,)), (far_b, 2, (1,)), (y_a, 3, (0,)), (y_b, 3, (1,))
    )


def spread_at_once(own):
    return ((own, 0, (0, 1)), (swap_x(own), 1, (0, 1)), (swap_far(own), 2, (0, 1)), (swap_y(own), 3, (0, 1)))


def body(gradient, signs, model):
    shares, lines, layers = (lax.axis_size(name) for name in ("shot", "inline", "depth"))
    planes, rows, cols = model.shape
    share = rows // shares
    sizes = (planes, planes * layers, rows * lines)
    paired = layers == 2
    at = gray(lax.axis_index("shot"))
    layer = lax.axis_index("depth")
    flip = (1 - layer) if paired else 0 * layer
    start_x = lax.axis_index("inline") * rows + at * share
    spot = jnp.stack([at, at ^ 1, at ^ 2, at ^ 3, flip, layer * planes, start_x]).astype(jnp.int32)

    order = [gray(place) * lines + line for line in range(lines) for place in range(shares)]
    ahead_x = list(zip(order[:-1], order[1:]))
    back_x = [(j, i) for i, j in ahead_x]
    ahead_z = [(i, i + 1) for i in range(layers - 1)]
    back_z = [(j, i) for i, j in ahead_z]

    def across(edges):
        tops, feet = edges
        group = ("shot", "inline")
        return lax.ppermute(tops, group, ahead_x), lax.ppermute(feet, group, back_x)

    gradient = pltpu.with_memory_space_constraint(gradient, pltpu.HBM)
    model = pltpu.with_memory_space_constraint(model, pltpu.HBM)
    signs = pltpu.with_memory_space_constraint(signs, pltpu.HBM)

    def both(a, b):
        return swap_x(a), swap_y(b)

    def crossed(a, b):
        return swap_y(a), swap_x(b)

    def prep(chunk, after=()):
        return prepare(chunk, spot, signs, gradient, shares, after)

    if not paired:
        c0 = (0, planes)
        sent = prep(c0)
        near = both(*sent)
        *fores, base = hold([c0], spot, signs, gradient, model, shares, sent)
        far = crossed(*relay(c0, fores, near))
        target = settle([c0], base, near, far)
        low = lax.ppermute(target[planes - HALO :], "depth", ahead_z)
        high = lax.ppermute(target[:HALO], "depth", back_z)
        before, after = across(pack((low, target, high)))
        pieces = [
            (0, HALO, 0, HALO, 0, 0, 0, 0),
            (1, planes, 0, planes, 0, HALO, HALO, 0),
            (2, HALO, 0, HALO, 0, HALO + planes, HALO + planes, 0),
        ]
        own = vary((0, planes), pieces, sizes, spot, (low, target, high), (before,), (after,))
        return gather((0, planes), spot, model.shape, spread(own))

    n0, n1 = ((7 * planes) // 16, planes // 4)
    n2 = planes - n0 - n1
    c0, c1, c2 = ((0, n0), (n0, n1), (n0 + n1, n2))
    sent_0 = prep(c0)
    near_0 = both(*sent_0)
    sent_1 = prep(c1, sent_0)
    near_1 = both(*sent_1)
    *fores, base = hold([c0, c1, c2], spot, signs, gradient, model, shares, sent_1)
    sent_2 = prep(c2, (base,))
    passed_0 = relay(c0, fores, near_0, after=sent_2)
    far_0 = crossed(*passed_0)
    passed_1 = relay(c1, fores, near_1, after=passed_0)
    near_2 = both(*idle(sent_2, passed_1))
    mid_0 = settle([c0], base, near_0, far_0, passed_1)
    edge = lax.dynamic_slice_in_dim(mid_0, turn(flip, 0, HALO, n0), HALO, 0)
    beside = lax.ppermute(edge, "depth", ahead_z + back_z)
    before_0, after_0 = across(pack((mid_0, beside)))
    passed_2 = relay(c2, fores, near_2, passed_1, (before_0, after_0))
    far_1 = crossed(*passed_2)
    mid_1 = settle([c1, c2], base, near_1 + near_2, far_1)
    before_1, after_1 = across(pack((mid_1,)))

    arrays = {"beside": beside, "mid_0": mid_0, "mid_1": mid_1}
    sides = [(before_0, after_0), (before_1, after_1)]
    held = [
        (-HALO, HALO, "beside", 0, 0, n0),
        (0, n0, "mid_0", 0, 0, 0),
        (n0, n1, "mid_1", 0, 1, 0),
        (n0 + n1, n2, "mid_1", n1, 1, n1),
        (planes, HALO, None, 0, 0, 0),
    ]

    def update(span, after=()):
        start, stop = (span[0] - HALO, span[1] + HALO)
        names, used, pieces = ([], [], [])
        for first, count, name, base, side, line in held:
            low, high = (max(first, start), min(first + count, stop))
            if low >= high:
                continue
            if name is not None:
                names += [name] if name not in names else []
                used += [side] if side not in used else []
            pieces.append((name, first, count, base, side, line, low, high))
        plan = []
        for name, first, count, base, side, line, low, high in pieces:
            if name is None:
                plan.append((None, 0, 0, high - low, 0, 0, low - start, 0))
            else:
                plan.append((names.index(name), count, low - first, high - low, used.index(side), line, low - start, base))
        return vary(
            span, plan, sizes, spot, [arrays[n] for n in names], [sides[i][0] for i in used], [sides[i][1] for i in used], after
        )

    m0 = n0 - HALO
    m1 = (m0 + planes) // 2
    spans = ((0, m0), (m0, m1), (m1, planes))
    own_0 = update(spans[0], passed_2)
    pieces_0 = spread(own_0)
    own_1 = update(spans[1], (own_0,))
    pieces_1 = spread(own_1)
    own_2 = update(spans[2], (own_1, pieces_0[1][0], pieces_0[4][0]))
    out = gather(spans[0], spot, model.shape, pieces_0)
    out = gather(spans[1], spot, model.shape, pieces_1, out)
    out = gather(spans[2], spot, model.shape, spread_halves(own_2), out)
    return out


def solution(mesh):
    placed = (P("shot", "depth", "inline", None), P("shot", None), P("depth", "inline", None))
    return jax.shard_map(
        body, mesh=mesh, in_specs=placed, out_specs=P("depth", "inline", None), check_vma=False
    )
```

```python
import functools

import jax
import jax.numpy as jnp
from jax import lax
from jax.experimental import pallas as pl
from jax.experimental.pallas import tpu as pltpu
from jax.sharding import PartitionSpec as P

ITERS = 3
HALO = 3
SIDE = 8
VMEM_LIMIT = 16 * 1024 * 1024

step_tau = 0.28
step_sigma = 0.28
radius = 0.3
rate = 0.5

keep_old = 1.0 / (1.0 + step_tau)
take_new = step_tau / (1.0 + step_tau)

PAIRS_X = [(0, 1), (1, 0), (2, 3), (3, 2)]
PAIRS_Y = [(0, 2), (2, 0), (1, 3), (3, 1)]
PAIRS_FAR = [(0, 3), (3, 0), (1, 2), (2, 1)]


def near_core(arrays):
    return [pltpu.with_memory_space_constraint(array, pltpu.VMEM) for array in arrays]


def swap_x(array):
    return lax.ppermute(array, "shot", PAIRS_X)


def swap_y(array):
    return lax.ppermute(array, "shot", PAIRS_Y)


def swap_far(array):
    return lax.ppermute(array, "shot", PAIRS_FAR)


def params():
    return pltpu.CompilerParams(vmem_limit_bytes=VMEM_LIMIT)


COST = pl.CostEstimate(flops=1, bytes_accessed=1, transcendentals=0)
HUGE = pl.CostEstimate(flops=1, bytes_accessed=1_000_000_000, transcendentals=0)
LONG = pl.CostEstimate(flops=1, bytes_accessed=100_000_000, transcendentals=0)


def tile_rows(rows):
    return slice(rows * SIDE, rows * SIDE + SIDE)


WHOLE = pl.BlockSpec(memory_space=pltpu.VMEM)
SCALARS = pl.BlockSpec(memory_space=pltpu.SMEM)
ANYWHERE = pl.BlockSpec(memory_space=pl.ANY)
FLIP, START_Z, START_X = (4, 5, 6)


def turn(flip, offset, count, total):
    return jnp.where(flip == 1, total - offset - count, offset)


def factor(signs):
    return (2 * signs[...] - 1).astype(jnp.float32)


def share_rows(spot, which, share):
    return pl.ds(pl.multiple_of(spot[which] * share, share), share)


def chunk_planes(spot, chunk, planes):
    offset, count = chunk
    return pl.ds(turn(spot[FLIP], offset, count, planes), count)


def fetch(source, spot, chunk, which, side, into, sem):
    planes, share, width = (source.shape[-3], into.shape[-2], into.shape[-1])
    place = (chunk_planes(spot, chunk, planes), share_rows(spot, which, share), pl.ds(side, width))
    if len(source.shape) == 4:
        place = (0,) + place
    copy = pltpu.make_async_copy(source.at[place], into, sem)
    copy.start()
    return copy


def prepare_kernel(chunk, after, spot, signs, gradient, *rest):
    out_a, out_b, held, held_signs, sems = rest[after:]
    half = out_a.shape[3]
    copy_signs = pltpu.make_async_copy(signs, held_signs, sems.at[4])
    copy_signs.start()
    todo = [(out_a, i, which, 0) for i, which in enumerate((1, 2))]
    todo += [(out_b, i, which, half) for i, which in enumerate((3, 2))]
    copies = [fetch(gradient, spot, chunk, which, side, held.at[n], sems.at[n]) for n, (_, _, which, side) in enumerate(todo)]
    copy_signs.wait()
    sign = factor(held_signs)[None]
    for n, (out, i, _, side) in enumerate(todo):
        copies[n].wait()
        out[i] = held[n] * sign[:, :, side : side + half]


def prepare(chunk, spot, signs, gradient, shares, after=(), keep=False):
    rows, cols = gradient.shape[2:]
    shape = (2, chunk[1], rows // shares, cols // 2)
    return pl.pallas_call(
        functools.partial(prepare_kernel, chunk, len(after)),
        in_specs=[SCALARS] + [ANYWHERE] * 2 + [WHOLE] * len(after),
        out_specs=[WHOLE] * 2,
        out_shape=[pltpu.VMEM(shape, jnp.float32) if keep else jax.ShapeDtypeStruct(shape, jnp.float32)] * 2,
        scratch_shapes=[
            pltpu.VMEM((4,) + shape[1:], jnp.float32),
            pltpu.VMEM(signs.shape, jnp.int32),
            pltpu.SemaphoreType.DMA((5,)),
        ],
        compiler_params=params(),
        cost_estimate=COST,
    )(spot, signs, gradient, *near_core(after))


def hold_kernel(chunks, after, spot, signs, gradient, model, *rest):
    fore_a, fore_b, base, held_a, held_b, held, held_signs, sems = rest[after:]
    half = fore_a.shape[2]
    copy_signs = pltpu.make_async_copy(signs, held_signs, sems.at[4 * len(chunks)])
    copy_signs.start()
    todo = []
    for chunk in chunks:
        here = pl.ds(*chunk)
        parts = ((gradient, 3, 0, held_a), (gradient, 1, half, held_b), (gradient, 0, 0, held.at[0]), (model, 0, 0, held.at[1]))
        copies = [
            fetch(source, spot, chunk, which, side, into.at[here], sems.at[len(todo) * 4 + n])
            for n, (source, which, side, into) in enumerate(parts)
        ]
        todo.append((copies, slice(chunk[0], chunk[0] + chunk[1])))
    copy_signs.wait()
    sign = factor(held_signs)[None]
    for copies, here in todo:
        for copy in copies:
            copy.wait()
        fore_a[here] = held_a[here] * sign[:, :, :half]
        fore_b[here] = held_b[here] * sign[:, :, half:]
        base[here] = held[1, here] - rate * (held[0, here] * sign)


def hold(chunks, spot, signs, gradient, model, shares, after=()):
    planes, rows, cols = model.shape
    whole = (planes, rows // shares, cols)
    part = (planes, rows // shares, cols // 2)
    return pl.pallas_call(
        functools.partial(hold_kernel, chunks, len(after)),
        in_specs=[SCALARS] + [ANYWHERE] * 3 + [WHOLE] * len(after),
        out_specs=[WHOLE] * 3,
        out_shape=[pltpu.VMEM(shape, jnp.float32) for shape in (part, part, whole)],
        scratch_shapes=[
            pltpu.VMEM(part, jnp.float32),
            pltpu.VMEM(part, jnp.float32),
            pltpu.VMEM((2,) + whole, jnp.float32),
            pltpu.VMEM(signs.shape, jnp.int32),
            pltpu.SemaphoreType.DMA((4 * len(chunks) + 1,)),
        ],
        compiler_params=params(),
        cost_estimate=COST,
    )(spot, signs, gradient, model, *near_core(after))


def relay_kernel(chunk, carried, ready, after, fore_a, fore_b, near_a, near_b, *rest):
    outs = rest[carried + ready + after :]
    here = slice(chunk[0], chunk[0] + chunk[1])
    at = 0
    if ready:
        at = rest[carried].shape[0]
        outs[0][:at] = rest[carried][...]
        outs[1][:at] = rest[carried + 1][...]
    outs[0][at:] = fore_a[here] + near_a[1]
    outs[1][at:] = fore_b[here] + near_b[1]
    for source, out in zip(rest[:carried], outs[2:]):
        out[...] = source[...]


def relay(chunk, fores, near, carried=(), after=(), ready=()):
    count = chunk[1] + sum(array.shape[0] for array in ready[:1])
    shapes = [(count,) + near[0].shape[2:]] * 2 + [array.shape for array in carried]
    outs = pl.pallas_call(
        functools.partial(relay_kernel, chunk, len(carried), len(ready), len(after)),
        in_specs=[WHOLE] * (4 + len(carried) + len(ready) + len(after)),
        out_specs=[WHOLE] * len(shapes),
        out_shape=[jax.ShapeDtypeStruct(shape, jnp.float32) for shape in shapes],
        compiler_params=params(),
        cost_estimate=COST,
    )(*fores, *near_core((*near, *carried, *ready, *after)))
    return outs[:2], outs[2:]


def settle_kernel(chunks, after, base, *refs):
    nears, (far_a, far_b) = (refs[: 2 * len(chunks)], refs[2 * len(chunks) : 2 * len(chunks) + 2])
    out = refs[-1]
    half = far_a.shape[2]
    at = 0
    for k, (start, count) in enumerate(chunks):
        here = slice(at, at + count)
        for side, near, far in ((slice(0, half), nears[2 * k], far_a), (slice(half, 2 * half), nears[2 * k + 1], far_b)):
            out[here, :, side] = base[start : start + count, :, side] - rate * (near[0] + far[here])
        at += count


def settle(chunks, base, nears, fars, after=()):
    count, share, half = fars[0].shape
    return pl.pallas_call(
        functools.partial(settle_kernel, chunks, len(after)),
        in_specs=[WHOLE] * (3 + len(nears)) + [WHOLE] * len(after),
        out_specs=WHOLE,
        out_shape=jax.ShapeDtypeStruct((count, share, 2 * half), jnp.float32),
        compiler_params=params(),
        cost_estimate=COST,
    )(base, *near_core((*nears, *fars, *after)))


def pack_kernel(count, spot, *refs):
    parts, (one, two) = (refs[:count], refs[count:])
    odd = spot[0] % 2 == 1
    at = 0
    for part in parts:
        for p in range(part.shape[0]):
            last = part[p, part.shape[1] - HALO :]
            first = part[p, :HALO]
            one[at] = jnp.where(odd, first, last)
            two[at] = jnp.where(odd, last, first)
            at += 1


def pack(spot, parts):
    shape = (sum(part.shape[0] for part in parts), HALO, parts[0].shape[2])
    return pl.pallas_call(
        functools.partial(pack_kernel, len(parts)),
        in_specs=[SCALARS] + [WHOLE] * len(parts),
        out_specs=[WHOLE] * 2,
        out_shape=[jax.ShapeDtypeStruct(shape, jnp.float32)] * 2,
        compiler_params=params(),
        cost_estimate=COST,
    )(spot, *near_core(parts))


def vary_kernel(span, pieces, sizes, counts, after, spot, *refs):
    fields, befores, afters = (refs[: counts[0]], refs[counts[0] : counts[0] + counts[1]], refs[counts[0] + counts[1] : counts[0] + 2 * counts[1]])
    out, target, primal, ahead, dual = refs[counts[0] + 2 * counts[1] + after :]
    planes, rows, cols = target.shape
    depth_planes, total_z, total_x = sizes
    share = rows - SIDE
    half = cols // 2
    tiles = share // SIDE
    shape = (SIDE, cols)
    flip = spot[FLIP]
    odd = spot[0] % 2 == 1

    for field, held, offset, count, side, line, there, base in pieces:
        goes = turn(flip, there, count, planes)
        if field is None:
            for i in range(count):
                target[goes + i] = jnp.zeros((rows, cols), jnp.float32)
            continue
        comes = turn(flip, offset, count, held)
        for i in range(count):
            target[goes + i, :share] = fields[field][base + comes + i]
            target[goes + i, share:rows] = jnp.zeros(shape, jnp.float32)
            one = befores[side][line + comes + i]
            two = afters[side][line + comes + i]
            target[goes + i, share : share + HALO] = jnp.where(odd, two, one)
            target[goes + i, rows - HALO : rows] = jnp.where(odd, one, two)

    row = lax.broadcasted_iota(jnp.int32, shape, 0)
    col = lax.broadcasted_iota(jnp.int32, shape, 1)
    first_row, last_row = (row == 0, row == SIDE - 1)
    coef_y = jnp.where(col < cols - 1, jnp.float32(step_sigma), jnp.float32(0))
    start_x = spot[START_X]
    start_z = spot[START_Z] + turn(flip, span[0] - HALO, planes, depth_planes)

    def coef_x(place):
        return jnp.where((place >= 0) & (place <= total_x - 2), jnp.float32(step_sigma), jnp.float32(0))

    edge_x = {
        tiles - 1: coef_x(start_x + share - SIDE + row),
        tiles: coef_x(start_x + jnp.where(row < SIDE // 2, share + row, row - SIDE)),
    }

    for step in range(ITERS):
        source = target if step == 0 else ahead
        old = target if step == 0 else primal

        def plane(p, carry):
            place = start_z + p
            coef_z = jnp.where((place >= 0) & (place <= total_z - 2), jnp.float32(step_sigma), jnp.float32(0))
            tile = [source[p, tile_rows(t)] for t in range(tiles + 1)]
            turned = [pltpu.roll(v, SIDE - 1, 0) for v in tile]

            def steps_of(t):
                here = tile_rows(t)
                v = tile[t]
                beyond = turned[(t + 1) % (tiles + 1)]
                step_z = coef_z * (source[p + 1, here] - v)
                step_x = edge_x.get(t, jnp.float32(step_sigma)) * (jnp.where(last_row, beyond, turned[t]) - v)
                step_y = coef_y * (pltpu.roll(v, cols - 1, 1) - v)
                if step > 0:
                    step_z = step_z + dual[0, p, here]
                    step_x = step_x + dual[1, p, here]
                    step_y = step_y + dual[2, p, here]
                square = step_z * step_z + step_x * step_x + step_y * step_y
                scale = jnp.minimum(jnp.float32(1), jnp.float32(radius) * lax.rsqrt(square))
                step_z, step_x, step_y = (step_z * scale, step_x * scale, step_y * scale)
                dual[0, p, here] = step_z
                if step < ITERS - 1:
                    dual[1, p, here] = step_x
                    dual[2, p, here] = step_y
                return step_z, step_x, step_y, pltpu.roll(step_x, 1, 0)

            def renew(t, steps, last_x):
                here = tile_rows(t)
                step_z, step_x, step_y, moved = steps
                diverge = (
                    (step_z - dual[0, jnp.maximum(p - 1, 0), here])
                    + (step_x - jnp.where(first_row, last_x, moved))
                    + (step_y - pltpu.roll(step_y, 1, 1))
                )
                before_it = old[p, here]
                fresh = jnp.float32(keep_old) * before_it + jnp.float32(take_new) * (diverge + target[p, here])
                if step < ITERS - 1:
                    primal[p, here] = fresh
                    ahead[p, here] = 2.0 * fresh - before_it
                else:
                    place_out = jnp.maximum(p - HALO, 0)
                    out[0, place_out, here] = fresh[:, :half]
                    out[1, place_out, here] = fresh[:, half:]

            edge_steps = steps_of(tiles)
            last_x = edge_steps[3]
            for t in range(tiles):
                steps = steps_of(t)
                renew(t, steps, last_x)
                last_x = steps[3]
            if step < ITERS - 1:
                renew(tiles, edge_steps, last_x)
            return carry

        lax.fori_loop(step, planes - 1 - step, plane, 0)


def vary(span, pieces, sizes, spot, fields, befores, afters, after=()):
    _, share, cols = fields[0].shape
    planes, rows = (span[1] - span[0] + 2 * HALO, share + SIDE)
    field = pltpu.VMEM((planes, rows, cols), jnp.float32)
    counts = (len(fields), len(befores))
    return pl.pallas_call(
        functools.partial(vary_kernel, span, pieces, sizes, counts, len(after)),
        in_specs=[SCALARS] + [WHOLE] * (counts[0] + 2 * counts[1]) + [WHOLE] * len(after),
        out_specs=WHOLE,
        out_shape=jax.ShapeDtypeStruct((2, span[1] - span[0], share, cols // 2), jnp.float32),
        scratch_shapes=[field, field, field, pltpu.VMEM((3, planes, rows, cols), jnp.float32)],
        compiler_params=params(),
        cost_estimate=LONG,
    )(spot, *near_core((*fields, *befores, *afters, *after)))


def gather_kernel(span, parts, spot, *refs):
    out, sems = refs[-2:]
    layers = chunk_planes(spot, (span[0], span[1] - span[0]), out.shape[0])
    copies = []
    for ref, (which, sides) in zip(refs, parts):
        share, half = ref.shape[-2:]
        for n, side in enumerate(sides):
            there = out.at[layers, share_rows(spot, which, share), pl.ds(side * half, half)]
            source = ref.at[n] if len(ref.shape) == 4 else ref
            copies.append(pltpu.make_async_copy(source, there, sems.at[len(copies)]))
    for copy in copies:
        copy.start()
    for copy in copies:
        copy.wait()


def gather(span, spot, out_shape, pieces, so_far=None, cost=COST):
    before = [] if so_far is None else [so_far]
    arrays, parts = zip(*((array, (which, sides)) for array, which, sides in pieces))
    return pl.pallas_call(
        functools.partial(gather_kernel, span, parts),
        in_specs=[SCALARS] + [ANYWHERE] * (len(arrays) + len(before)),
        out_specs=pl.BlockSpec(memory_space=pltpu.HBM),
        out_shape=jax.ShapeDtypeStruct(out_shape, jnp.float32),
        input_output_aliases={1 + len(arrays): 0} if before else {},
        scratch_shapes=[pltpu.SemaphoreType.DMA((8,))],
        compiler_params=params(),
        cost_estimate=cost,
    )(spot, *arrays, *before)


def carry_kernel(count, after, *refs):
    for source, out in zip(refs[:count], refs[count + after :]):
        out[...] = source[...]


def carry(arrays, after):
    return pl.pallas_call(
        functools.partial(carry_kernel, len(arrays), len(after)),
        in_specs=[WHOLE] * (len(arrays) + len(after)),
        out_specs=[WHOLE] * len(arrays),
        out_shape=[jax.ShapeDtypeStruct(array.shape, array.dtype) for array in arrays],
        compiler_params=params(),
        cost_estimate=COST,
    )(*near_core((*arrays, *after)))


def gray(place):
    return place ^ (place >> 1)


def spread(own):
    from_x, from_y = (swap_x(own), swap_y(own))
    far_a, far_b = (swap_x(from_y[0]), swap_y(from_x[1]))
    return ((own, 0, (0, 1)), (from_x, 1, (0, 1)), (far_a, 2, (0,)), (far_b, 2, (1,)), (from_y, 3, (0, 1)))


def spread_halves(own):
    y_a, x_b = (swap_y(own[0]), swap_x(own[1]))
    x_a, y_b = (swap_x(own[0]), swap_y(own[1]))
    far_a, far_b = (swap_x(y_a), swap_y(x_b))
    return (
        (own, 0, (0, 1)), (x_a, 1, (0,)), (x_b, 1, (1,)), (far_a, 2, (0,)), (far_b, 2, (1,)), (y_a, 3, (0,)), (y_b, 3, (1,))
    )


def spread_at_once(own):
    return ((own, 0, (0, 1)), (swap_x(own), 1, (0, 1)), (swap_far(own), 2, (0, 1)), (swap_y(own), 3, (0, 1)))


def body(gradient, signs, model):
    shares, lines, layers = (lax.axis_size(name) for name in ("shot", "inline", "depth"))
    planes, rows, cols = model.shape
    share = rows // shares
    sizes = (planes, planes * layers, rows * lines)
    paired = layers == 2
    at = gray(lax.axis_index("shot"))
    layer = lax.axis_index("depth")
    flip = (1 - layer) if paired else 0 * layer
    start_x = lax.axis_index("inline") * rows + at * share
    spot = jnp.stack([at, at ^ 1, at ^ 2, at ^ 3, flip, layer * planes, start_x]).astype(jnp.int32)

    order = [gray(place) * lines + line for line in range(lines) for place in range(shares)]
    pairs_one = [pair for i, j in zip(order[::2], order[1::2]) for pair in ((i, j), (j, i))]
    pairs_two = [pair for i, j in zip(order[1:-1:2], order[2::2]) for pair in ((i, j), (j, i))]
    ahead_z = [(i, i + 1) for i in range(layers - 1)]
    back_z = [(j, i) for i, j in ahead_z]

    def across(edges):
        group = ("shot", "inline")
        return [lax.ppermute(edge, group, pairs) for edge, pairs in zip(edges, (pairs_one, pairs_two))]

    gradient = pltpu.with_memory_space_constraint(gradient, pltpu.HBM)
    model = pltpu.with_memory_space_constraint(model, pltpu.HBM)
    signs = pltpu.with_memory_space_constraint(signs, pltpu.HBM)

    def both(a, b):
        return swap_x(a), swap_y(b)

    def crossed(a, b):
        return swap_y(a), swap_x(b)

    def prep(chunk, after=()):
        return prepare(chunk, spot, signs, gradient, shares, after)

    if not paired:
        c0 = (0, planes)
        sent = prep(c0)
        near = both(*sent)
        *fores, base = hold([c0], spot, signs, gradient, model, shares, sent)
        far = crossed(*relay(c0, fores, near)[0])
        target = settle([c0], base, near, far)
        low = lax.ppermute(target[planes - HALO :], "depth", ahead_z)
        high = lax.ppermute(target[:HALO], "depth", back_z)
        before, after = across(pack(spot, (low, target, high)))
        pieces = [
            (0, HALO, 0, HALO, 0, 0, 0, 0),
            (1, planes, 0, planes, 0, HALO, HALO, 0),
            (2, HALO, 0, HALO, 0, HALO + planes, HALO + planes, 0),
        ]
        own = vary((0, planes), pieces, sizes, spot, (low, target, high), (before,), (after,))
        return gather((0, planes), spot, model.shape, spread(own))

    n0, n1 = ((7 * planes) // 16, planes // 4)
    n2 = planes - n0 - n1
    c0, c1, c2 = ((0, n0), (n0, n1), (n0 + n1, n2))
    sent_0 = prep(c0)
    near_0 = both(*sent_0)
    sent_1 = prep(c1, sent_0)
    near_1 = both(*sent_1)
    *fores, base = hold([c0, c1, c2], spot, signs, gradient, model, shares, sent_1)
    sent_2 = prepare(c2, spot, signs, gradient, shares, (base,), True)
    passed_0, _ = relay(c0, fores, near_0, after=sent_2)
    far_0 = crossed(*passed_0)
    passed_1, sent_2 = relay(c1, fores, near_1, sent_2, passed_0)
    near_2 = both(*sent_2)
    mid_0 = settle([c0], base, near_0, far_0, passed_1)
    edge = lax.dynamic_slice_in_dim(mid_0, turn(flip, 0, HALO, n0), HALO, 0)
    beside = lax.ppermute(edge, "depth", ahead_z + back_z)
    edges_0 = pack(spot, (mid_0, beside))
    before_0, after_0 = across(edges_0)
    passed_2, _ = relay(c2, fores, near_2, after=edges_0, ready=passed_1)
    far_1 = crossed(*passed_2)
    arrays = {"beside": beside, "mid_0": mid_0, }
    sides = [(before_0, after_0)]
    held = [
        (-HALO, HALO, "beside", 0, 0, n0),
        (0, n0, "mid_0", 0, 0, 0),
        (n0, n1, "mid_1", 0, 1, 0),
        (n0 + n1, n2, "mid_1", n1, 1, n1),
        (planes, HALO, None, 0, 0, 0),
    ]

    def update(span, after=()):
        start, stop = (span[0] - HALO, span[1] + HALO)
        names, used, pieces = ([], [], [])
        for first, count, name, base, side, line in held:
            low, high = (max(first, start), min(first + count, stop))
            if low >= high:
                continue
            if name is not None:
                names += [name] if name not in names else []
                used += [side] if side not in used else []
            pieces.append((name, first, count, base, side, line, low, high))
        plan = []
        for name, first, count, base, side, line, low, high in pieces:
            if name is None:
                plan.append((None, 0, 0, high - low, 0, 0, low - start, 0))
            else:
                plan.append((names.index(name), count, low - first, high - low, used.index(side), line, low - start, base))
        return vary(
            span, plan, sizes, spot, [arrays[n] for n in names], [sides[i][0] for i in used], [sides[i][1] for i in used], after
        )

    m0 = n0 - HALO
    m1 = (m0 + planes) // 2
    spans = ((0, m0), (m0, m1), (m1, planes))
    own_0 = update(spans[0], passed_2)
    mid_1 = settle([c1, c2], base, near_1 + near_2, far_1, (own_0,))
    edges_1 = pack(spot, (mid_1,))
    before_1, after_1 = across(edges_1)
    arrays["mid_1"] = mid_1
    sides.append((before_1, after_1))
    pieces_0 = spread(own_0)
    own_1 = update(spans[1], (own_0,))
    pieces_1 = spread(own_1)
    own_2 = update(spans[2], (own_1, pieces_0[1][0], pieces_0[4][0]))
    out = gather(spans[0], spot, model.shape, pieces_0)
    out = gather(spans[1], spot, model.shape, pieces_1, out)
    out = gather(spans[2], spot, model.shape, spread_halves(own_2), out)
    return out


def solution(mesh):
    placed = (P("shot", "depth", "inline", None), P("shot", None), P("depth", "inline", None))
    return jax.shard_map(
        body, mesh=mesh, in_specs=placed, out_specs=P("depth", "inline", None), check_vma=False
    )
```

```python
import functools

import jax
import jax.numpy as jnp
from jax import lax
from jax.experimental import pallas as pl
from jax.experimental.pallas import tpu as pltpu
from jax.sharding import PartitionSpec as P

ITERS = 3
HALO = 3
SIDE = 8
VMEM_LIMIT = 16 * 1024 * 1024

step_tau = 0.28
step_sigma = 0.28
radius = 0.3
rate = 0.5

keep_old = 1.0 / (1.0 + step_tau)
take_new = step_tau / (1.0 + step_tau)

PAIRS_X = [(0, 1), (1, 0), (2, 3), (3, 2)]
PAIRS_Y = [(0, 2), (2, 0), (1, 3), (3, 1)]
PAIRS_FAR = [(0, 3), (3, 0), (1, 2), (2, 1)]


def near_core(arrays):
    return [pltpu.with_memory_space_constraint(array, pltpu.VMEM) for array in arrays]


def swap_x(array):
    return lax.ppermute(array, "shot", PAIRS_X)


def swap_y(array):
    return lax.ppermute(array, "shot", PAIRS_Y)


def swap_far(array):
    return lax.ppermute(array, "shot", PAIRS_FAR)


def params():
    return pltpu.CompilerParams(vmem_limit_bytes=VMEM_LIMIT)


COST = pl.CostEstimate(flops=1, bytes_accessed=1, transcendentals=0)
HUGE = pl.CostEstimate(flops=1, bytes_accessed=1_000_000_000, transcendentals=0)
LONG = pl.CostEstimate(flops=1, bytes_accessed=100_000_000, transcendentals=0)


def tile_rows(rows):
    return slice(rows * SIDE, rows * SIDE + SIDE)


WHOLE = pl.BlockSpec(memory_space=pltpu.VMEM)
SCALARS = pl.BlockSpec(memory_space=pltpu.SMEM)
ANYWHERE = pl.BlockSpec(memory_space=pl.ANY)
FLIP, START_Z, START_X = (4, 5, 6)


def turn(flip, offset, count, total):
    return jnp.where(flip == 1, total - offset - count, offset)


def factor(signs):
    return (2 * signs[...] - 1).astype(jnp.float32)


def share_rows(spot, which, share):
    return pl.ds(pl.multiple_of(spot[which] * share, share), share)


def chunk_planes(spot, chunk, planes):
    offset, count = chunk
    return pl.ds(turn(spot[FLIP], offset, count, planes), count)


def fetch(source, spot, chunk, which, side, into, sem):
    planes, share, width = (source.shape[-3], into.shape[-2], into.shape[-1])
    place = (chunk_planes(spot, chunk, planes), share_rows(spot, which, share), pl.ds(side, width))
    if len(source.shape) == 4:
        place = (0,) + place
    copy = pltpu.make_async_copy(source.at[place], into, sem)
    copy.start()
    return copy


def prepare_kernel(chunk, after, spot, signs, gradient, *rest):
    out_a, out_b, held, held_signs, sems = rest[after:]
    half = out_a.shape[3]
    copy_signs = pltpu.make_async_copy(signs, held_signs, sems.at[4])
    copy_signs.start()
    todo = [(out_a, i, which, 0) for i, which in enumerate((1, 2))]
    todo += [(out_b, i, which, half) for i, which in enumerate((3, 2))]
    copies = [fetch(gradient, spot, chunk, which, side, held.at[n], sems.at[n]) for n, (_, _, which, side) in enumerate(todo)]
    copy_signs.wait()
    sign = factor(held_signs)[None]
    for n, (out, i, _, side) in enumerate(todo):
        copies[n].wait()
        out[i] = held[n] * sign[:, :, side : side + half]


def prepare(chunk, spot, signs, gradient, shares, after=(), keep=False):
    rows, cols = gradient.shape[2:]
    shape = (2, chunk[1], rows // shares, cols // 2)
    return pl.pallas_call(
        functools.partial(prepare_kernel, chunk, len(after)),
        in_specs=[SCALARS] + [ANYWHERE] * 2 + [WHOLE] * len(after),
        out_specs=[WHOLE] * 2,
        out_shape=[pltpu.VMEM(shape, jnp.float32) if keep else jax.ShapeDtypeStruct(shape, jnp.float32)] * 2,
        scratch_shapes=[
            pltpu.VMEM((4,) + shape[1:], jnp.float32),
            pltpu.VMEM(signs.shape, jnp.int32),
            pltpu.SemaphoreType.DMA((5,)),
        ],
        compiler_params=params(),
        cost_estimate=COST,
    )(spot, signs, gradient, *near_core(after))


def hold_kernel(chunks, after, spot, signs, gradient, model, *rest):
    fore_a, fore_b, base, held_a, held_b, held, held_signs, sems = rest[after:]
    half = fore_a.shape[2]
    copy_signs = pltpu.make_async_copy(signs, held_signs, sems.at[4 * len(chunks)])
    copy_signs.start()
    todo = []
    for chunk in chunks:
        here = pl.ds(*chunk)
        parts = ((gradient, 3, 0, held_a), (gradient, 1, half, held_b), (gradient, 0, 0, held.at[0]), (model, 0, 0, held.at[1]))
        copies = [
            fetch(source, spot, chunk, which, side, into.at[here], sems.at[len(todo) * 4 + n])
            for n, (source, which, side, into) in enumerate(parts)
        ]
        todo.append((copies, slice(chunk[0], chunk[0] + chunk[1])))
    copy_signs.wait()
    sign = factor(held_signs)[None]
    for copies, here in todo:
        for copy in copies:
            copy.wait()
        fore_a[here] = held_a[here] * sign[:, :, :half]
        fore_b[here] = held_b[here] * sign[:, :, half:]
        base[here] = held[1, here] - rate * (held[0, here] * sign)


def hold(chunks, spot, signs, gradient, model, shares, after=()):
    planes, rows, cols = model.shape
    whole = (planes, rows // shares, cols)
    part = (planes, rows // shares, cols // 2)
    return pl.pallas_call(
        functools.partial(hold_kernel, chunks, len(after)),
        in_specs=[SCALARS] + [ANYWHERE] * 3 + [WHOLE] * len(after),
        out_specs=[WHOLE] * 3,
        out_shape=[pltpu.VMEM(shape, jnp.float32) for shape in (part, part, whole)],
        scratch_shapes=[
            pltpu.VMEM(part, jnp.float32),
            pltpu.VMEM(part, jnp.float32),
            pltpu.VMEM((2,) + whole, jnp.float32),
            pltpu.VMEM(signs.shape, jnp.int32),
            pltpu.SemaphoreType.DMA((4 * len(chunks) + 1,)),
        ],
        compiler_params=params(),
        cost_estimate=COST,
    )(spot, signs, gradient, model, *near_core(after))


def relay_kernel(chunk, carried, ready, after, fore_a, fore_b, near_a, near_b, *rest):
    outs = rest[carried + ready + after :]
    here = slice(chunk[0], chunk[0] + chunk[1])
    at = 0
    if ready:
        at = rest[carried].shape[0]
        outs[0][:at] = rest[carried][...]
        outs[1][:at] = rest[carried + 1][...]
    outs[0][at:] = fore_a[here] + near_a[1]
    outs[1][at:] = fore_b[here] + near_b[1]
    for source, out in zip(rest[:carried], outs[2:]):
        out[...] = source[...]


def relay(chunk, fores, near, carried=(), after=(), ready=()):
    count = chunk[1] + sum(array.shape[0] for array in ready[:1])
    shapes = [(count,) + near[0].shape[2:]] * 2 + [array.shape for array in carried]
    outs = pl.pallas_call(
        functools.partial(relay_kernel, chunk, len(carried), len(ready), len(after)),
        in_specs=[WHOLE] * (4 + len(carried) + len(ready) + len(after)),
        out_specs=[WHOLE] * len(shapes),
        out_shape=[jax.ShapeDtypeStruct(shape, jnp.float32) for shape in shapes],
        compiler_params=params(),
        cost_estimate=COST,
    )(*fores, *near_core((*near, *carried, *ready, *after)))
    return outs[:2], outs[2:]


def settle_kernel(chunks, edges, after, spot, base, *refs):
    nears, (far_a, far_b) = (refs[: 2 * len(chunks)], refs[2 * len(chunks) : 2 * len(chunks) + 2])
    out, *sides = refs[2 * len(chunks) + 2 + after :]
    half = far_a.shape[2]
    at = 0
    for k, (start, count) in enumerate(chunks):
        here = slice(at, at + count)
        for side, near, far in ((slice(0, half), nears[2 * k], far_a), (slice(half, 2 * half), nears[2 * k + 1], far_b)):
            out[here, :, side] = base[start : start + count, :, side] - rate * (near[0] + far[here])
        at += count
    if edges:
        odd = spot[0] % 2 == 1
        for p in range(out.shape[0]):
            last = out[p, out.shape[1] - HALO :]
            first = out[p, :HALO]
            sides[0][p] = jnp.where(odd, first, last)
            sides[1][p] = jnp.where(odd, last, first)


def settle(chunks, spot, base, nears, fars, after=(), edges=False):
    count, share, half = fars[0].shape
    shapes = [(count, share, 2 * half)] + ([(count, HALO, 2 * half)] * 2 if edges else [])
    return pl.pallas_call(
        functools.partial(settle_kernel, chunks, edges, len(after)),
        in_specs=[SCALARS] + [WHOLE] * (3 + len(nears) + len(after)),
        out_specs=[WHOLE] * len(shapes),
        out_shape=[jax.ShapeDtypeStruct(shape, jnp.float32) for shape in shapes],
        compiler_params=params(),
        cost_estimate=COST,
    )(spot, base, *near_core((*nears, *fars, *after)))


def pack_kernel(count, spot, *refs):
    parts, (one, two) = (refs[:count], refs[count:])
    odd = spot[0] % 2 == 1
    at = 0
    for part in parts:
        for p in range(part.shape[0]):
            last = part[p, part.shape[1] - HALO :]
            first = part[p, :HALO]
            one[at] = jnp.where(odd, first, last)
            two[at] = jnp.where(odd, last, first)
            at += 1


def pack(spot, parts):
    shape = (sum(part.shape[0] for part in parts), HALO, parts[0].shape[2])
    return pl.pallas_call(
        functools.partial(pack_kernel, len(parts)),
        in_specs=[SCALARS] + [WHOLE] * len(parts),
        out_specs=[WHOLE] * 2,
        out_shape=[jax.ShapeDtypeStruct(shape, jnp.float32)] * 2,
        compiler_params=params(),
        cost_estimate=COST,
    )(spot, *near_core(parts))


def vary_kernel(span, pieces, sizes, counts, after, spot, *refs):
    fields, befores, afters = (refs[: counts[0]], refs[counts[0] : counts[0] + counts[1]], refs[counts[0] + counts[1] : counts[0] + 2 * counts[1]])
    out, target, primal, ahead, dual = refs[counts[0] + 2 * counts[1] + after :]
    planes, rows, cols = target.shape
    depth_planes, total_z, total_x = sizes
    share = rows - SIDE
    half = cols // 2
    tiles = share // SIDE
    shape = (SIDE, cols)
    flip = spot[FLIP]
    odd = spot[0] % 2 == 1

    for field, held, offset, count, side, line, there, base in pieces:
        goes = turn(flip, there, count, planes)
        if field is None:
            for i in range(count):
                target[goes + i] = jnp.zeros((rows, cols), jnp.float32)
            continue
        comes = turn(flip, offset, count, held)
        for i in range(count):
            target[goes + i, :share] = fields[field][base + comes + i]
            target[goes + i, share:rows] = jnp.zeros(shape, jnp.float32)
            one = befores[side][line + comes + i]
            two = afters[side][line + comes + i]
            target[goes + i, share : share + HALO] = jnp.where(odd, two, one)
            target[goes + i, rows - HALO : rows] = jnp.where(odd, one, two)

    row = lax.broadcasted_iota(jnp.int32, shape, 0)
    col = lax.broadcasted_iota(jnp.int32, shape, 1)
    first_row, last_row = (row == 0, row == SIDE - 1)
    coef_y = jnp.where(col < cols - 1, jnp.float32(step_sigma), jnp.float32(0))
    start_x = spot[START_X]
    start_z = spot[START_Z] + turn(flip, span[0] - HALO, planes, depth_planes)

    def coef_x(place):
        return jnp.where((place >= 0) & (place <= total_x - 2), jnp.float32(step_sigma), jnp.float32(0))

    edge_x = {
        tiles - 1: coef_x(start_x + share - SIDE + row),
        tiles: coef_x(start_x + jnp.where(row < SIDE // 2, share + row, row - SIDE)),
    }

    for step in range(ITERS):
        source = target if step == 0 else ahead
        old = target if step == 0 else primal

        def plane(p, carry):
            place = start_z + p
            coef_z = jnp.where((place >= 0) & (place <= total_z - 2), jnp.float32(step_sigma), jnp.float32(0))
            rows_of = [tile_rows(t) for t in range(tiles + 1)]
            tile = [source[p, here] for here in rows_of]
            below = [source[p + 1, here] for here in rows_of]
            before_z = [dual[0, max(p - 1, 0), here] for here in rows_of]
            if step > 0:
                olds = [[dual[i, p, here] for here in rows_of] for i in range(3)]
                old_value = [old[p, here] for here in rows_of]
                goal = [target[p, here] for here in rows_of]
            else:
                old_value, goal = (tile, tile)
            turned = [pltpu.roll(v, SIDE - 1, 0) for v in tile]
            aside = [pltpu.roll(v, cols - 1, 1) for v in tile]
            all_steps = []
            for t in range(tiles + 1):
                v = tile[t]
                beyond = turned[(t + 1) % (tiles + 1)]
                step_z = coef_z * (below[t] - v)
                step_x = edge_x.get(t, jnp.float32(step_sigma)) * (jnp.where(last_row, beyond, turned[t]) - v)
                step_y = coef_y * (aside[t] - v)
                if step > 0:
                    step_z = step_z + olds[0][t]
                    step_x = step_x + olds[1][t]
                    step_y = step_y + olds[2][t]
                square = step_z * step_z + step_x * step_x + step_y * step_y
                scale = jnp.minimum(jnp.float32(1), jnp.float32(radius) * lax.rsqrt(square))
                all_steps.append((step_z * scale, step_x * scale, step_y * scale))
            moved = [pltpu.roll(steps[1], 1, 0) for steps in all_steps]
            aside = [pltpu.roll(steps[2], 1, 1) for steps in all_steps]
            news = []
            needed = 0 if p == step else tiles + 1 if step < ITERS - 1 else tiles
            for t in range(needed):
                step_z, step_x, step_y = all_steps[t]
                last_x = moved[t - 1 if t else tiles]
                diverge = (step_z - before_z[t]) + (step_x - jnp.where(first_row, last_x, moved[t])) + (step_y - aside[t])
                news.append(jnp.float32(keep_old) * old_value[t] + jnp.float32(take_new) * (diverge + goal[t]))
            for t, here in enumerate(rows_of):
                dual[0, p, here] = all_steps[t][0]
                if p == step:
                    continue
                if step < ITERS - 1:
                    dual[1, p, here] = all_steps[t][1]
                    dual[2, p, here] = all_steps[t][2]
                    primal[p, here] = news[t]
                    ahead[p, here] = 2.0 * news[t] - old_value[t]
                elif t < tiles:
                    place_out = max(p - HALO, 0)
                    out[0, place_out, here] = news[t][:, :half]
                    out[1, place_out, here] = news[t][:, half:]
            return carry

        for p in range(step, planes - 1 - step):
            plane(p, 0)


def vary(span, pieces, sizes, spot, fields, befores, afters, after=()):
    _, share, cols = fields[0].shape
    planes, rows = (span[1] - span[0] + 2 * HALO, share + SIDE)
    field = pltpu.VMEM((planes, rows, cols), jnp.float32)
    counts = (len(fields), len(befores))
    return pl.pallas_call(
        functools.partial(vary_kernel, span, pieces, sizes, counts, len(after)),
        in_specs=[SCALARS] + [WHOLE] * (counts[0] + 2 * counts[1]) + [WHOLE] * len(after),
        out_specs=WHOLE,
        out_shape=jax.ShapeDtypeStruct((2, span[1] - span[0], share, cols // 2), jnp.float32),
        scratch_shapes=[field, field, field, pltpu.VMEM((3, planes, rows, cols), jnp.float32)],
        compiler_params=params(),
        cost_estimate=LONG,
    )(spot, *near_core((*fields, *befores, *afters, *after)))


def gather_kernel(span, parts, spot, *refs):
    out, sems = refs[-2:]
    layers = chunk_planes(spot, (span[0], span[1] - span[0]), out.shape[0])
    copies = []
    for ref, (which, sides) in zip(refs, parts):
        share, half = ref.shape[-2:]
        for n, side in enumerate(sides):
            there = out.at[layers, share_rows(spot, which, share), pl.ds(side * half, half)]
            source = ref.at[n] if len(ref.shape) == 4 else ref
            copies.append(pltpu.make_async_copy(source, there, sems.at[len(copies)]))
    for copy in copies:
        copy.start()
    for copy in copies:
        copy.wait()


def gather(span, spot, out_shape, pieces, so_far=None, cost=COST):
    before = [] if so_far is None else [so_far]
    arrays, parts = zip(*((array, (which, sides)) for array, which, sides in pieces))
    return pl.pallas_call(
        functools.partial(gather_kernel, span, parts),
        in_specs=[SCALARS] + [ANYWHERE] * (len(arrays) + len(before)),
        out_specs=pl.BlockSpec(memory_space=pltpu.HBM),
        out_shape=jax.ShapeDtypeStruct(out_shape, jnp.float32),
        input_output_aliases={1 + len(arrays): 0} if before else {},
        scratch_shapes=[pltpu.SemaphoreType.DMA((8,))],
        compiler_params=params(),
        cost_estimate=cost,
    )(spot, *arrays, *before)


def carry_kernel(count, after, *refs):
    for source, out in zip(refs[:count], refs[count + after :]):
        out[...] = source[...]


def carry(arrays, after):
    return pl.pallas_call(
        functools.partial(carry_kernel, len(arrays), len(after)),
        in_specs=[WHOLE] * (len(arrays) + len(after)),
        out_specs=[WHOLE] * len(arrays),
        out_shape=[jax.ShapeDtypeStruct(array.shape, array.dtype) for array in arrays],
        compiler_params=params(),
        cost_estimate=COST,
    )(*near_core((*arrays, *after)))


def gray(place):
    return place ^ (place >> 1)


def spread(own):
    from_x, from_y = (swap_x(own), swap_y(own))
    far_a, far_b = (swap_x(from_y[0]), swap_y(from_x[1]))
    return ((own, 0, (0, 1)), (from_x, 1, (0, 1)), (far_a, 2, (0,)), (far_b, 2, (1,)), (from_y, 3, (0, 1)))


def spread_halves(own):
    y_a, x_b = (swap_y(own[0]), swap_x(own[1]))
    x_a, y_b = (swap_x(own[0]), swap_y(own[1]))
    far_a, far_b = (swap_x(y_a), swap_y(x_b))
    return (
        (own, 0, (0, 1)), (x_a, 1, (0,)), (x_b, 1, (1,)), (far_a, 2, (0,)), (far_b, 2, (1,)), (y_a, 3, (0,)), (y_b, 3, (1,))
    )


def spread_at_once(own):
    return ((own, 0, (0, 1)), (swap_x(own), 1, (0, 1)), (swap_far(own), 2, (0, 1)), (swap_y(own), 3, (0, 1)))


def body(gradient, signs, model):
    shares, lines, layers = (lax.axis_size(name) for name in ("shot", "inline", "depth"))
    planes, rows, cols = model.shape
    share = rows // shares
    sizes = (planes, planes * layers, rows * lines)
    paired = layers == 2
    at = gray(lax.axis_index("shot"))
    layer = lax.axis_index("depth")
    flip = (1 - layer) if paired else 0 * layer
    start_x = lax.axis_index("inline") * rows + at * share
    spot = jnp.stack([at, at ^ 1, at ^ 2, at ^ 3, flip, layer * planes, start_x]).astype(jnp.int32)

    order = [gray(place) * lines + line for line in range(lines) for place in range(shares)]
    pairs_one = [pair for i, j in zip(order[::2], order[1::2]) for pair in ((i, j), (j, i))]
    pairs_two = [pair for i, j in zip(order[1:-1:2], order[2::2]) for pair in ((i, j), (j, i))]
    ahead_z = [(i, i + 1) for i in range(layers - 1)]
    back_z = [(j, i) for i, j in ahead_z]

    def across(edges):
        group = ("shot", "inline")
        return [lax.ppermute(edge, group, pairs) for edge, pairs in zip(edges, (pairs_one, pairs_two))]

    gradient = pltpu.with_memory_space_constraint(gradient, pltpu.HBM)
    model = pltpu.with_memory_space_constraint(model, pltpu.HBM)
    signs = pltpu.with_memory_space_constraint(signs, pltpu.HBM)

    def both(a, b):
        return swap_x(a), swap_y(b)

    def crossed(a, b):
        return swap_y(a), swap_x(b)

    def prep(chunk, after=()):
        return prepare(chunk, spot, signs, gradient, shares, after)

    if not paired:
        c0 = (0, planes)
        sent = prep(c0)
        near = both(*sent)
        *fores, base = hold([c0], spot, signs, gradient, model, shares, sent)
        far = crossed(*relay(c0, fores, near)[0])
        (target,) = settle([c0], spot, base, near, far)
        low = lax.ppermute(target[planes - HALO :], "depth", ahead_z)
        high = lax.ppermute(target[:HALO], "depth", back_z)
        before, after = across(pack(spot, (low, target, high)))
        pieces = [
            (0, HALO, 0, HALO, 0, 0, 0, 0),
            (1, planes, 0, planes, 0, HALO, HALO, 0),
            (2, HALO, 0, HALO, 0, HALO + planes, HALO + planes, 0),
        ]
        own = vary((0, planes), pieces, sizes, spot, (low, target, high), (before,), (after,))
        return gather((0, planes), spot, model.shape, spread(own))

    n0, n1 = ((7 * planes) // 16, planes // 4)
    n2 = planes - n0 - n1
    c0, c1, c2 = ((0, n0), (n0, n1), (n0 + n1, n2))
    sent_0 = prep(c0)
    near_0 = both(*sent_0)
    sent_1 = prep(c1, sent_0)
    near_1 = both(*sent_1)
    *fores, base = hold([c0, c1, c2], spot, signs, gradient, model, shares, sent_1)
    sent_2 = prepare(c2, spot, signs, gradient, shares, (base,), True)
    passed_0, _ = relay(c0, fores, near_0, after=sent_2)
    far_0 = crossed(*passed_0)
    passed_1, sent_2 = relay(c1, fores, near_1, sent_2, passed_0)
    near_2 = both(*sent_2)
    (mid_0,) = settle([c0], spot, base, near_0, far_0, passed_1)
    edge = lax.dynamic_slice_in_dim(mid_0, turn(flip, 0, HALO, n0), HALO, 0)
    beside = lax.ppermute(edge, "depth", ahead_z + back_z)
    edges_0 = pack(spot, (mid_0, beside))
    before_0, after_0 = across(edges_0)
    passed_2, _ = relay(c2, fores, near_2, after=edges_0, ready=passed_1)
    far_1 = crossed(*passed_2)
    arrays = {"beside": beside, "mid_0": mid_0, }
    sides = [(before_0, after_0)]
    held = [
        (-HALO, HALO, "beside", 0, 0, n0),
        (0, n0, "mid_0", 0, 0, 0),
        (n0, n1, "mid_1", 0, 1, 0),
        (n0 + n1, n2, "mid_1", n1, 1, n1),
        (planes, HALO, None, 0, 0, 0),
    ]

    def update(span, after=()):
        start, stop = (span[0] - HALO, span[1] + HALO)
        names, used, pieces = ([], [], [])
        for first, count, name, base, side, line in held:
            low, high = (max(first, start), min(first + count, stop))
            if low >= high:
                continue
            if name is not None:
                names += [name] if name not in names else []
                used += [side] if side not in used else []
            pieces.append((name, first, count, base, side, line, low, high))
        plan = []
        for name, first, count, base, side, line, low, high in pieces:
            if name is None:
                plan.append((None, 0, 0, high - low, 0, 0, low - start, 0))
            else:
                plan.append((names.index(name), count, low - first, high - low, used.index(side), line, low - start, base))
        return vary(
            span, plan, sizes, spot, [arrays[n] for n in names], [sides[i][0] for i in used], [sides[i][1] for i in used], after
        )

    m0 = n0 - HALO
    m1 = (m0 + planes) // 2
    spans = ((0, m0), (m0, m1), (m1, planes))
    own_0 = update(spans[0], passed_2)
    mid_1, *edges_1 = settle([c1, c2], spot, base, near_1 + near_2, far_1, (own_0,), True)
    before_1, after_1 = across(edges_1)
    arrays["mid_1"] = mid_1
    sides.append((before_1, after_1))
    pieces_0 = spread(own_0)
    own_1 = update(spans[1], (own_0,))
    pieces_1 = spread(own_1)
    own_2 = update(spans[2], (own_1, pieces_0[1][0], pieces_0[4][0]))
    out = gather(spans[0], spot, model.shape, pieces_0)
    out = gather(spans[1], spot, model.shape, pieces_1, out)
    out = gather(spans[2], spot, model.shape, spread_halves(own_2), out)
    return out


def solution(mesh):
    placed = (P("shot", "depth", "inline", None), P("shot", None), P("depth", "inline", None))
    return jax.shard_map(
        body, mesh=mesh, in_specs=placed, out_specs=P("depth", "inline", None), check_vma=False
    )
```

```python
import functools

import jax
import jax.numpy as jnp
from jax import lax
from jax.experimental import pallas as pl
from jax.experimental.pallas import tpu as pltpu
from jax.sharding import PartitionSpec as P

ITERS = 3
HALO = 3
SIDE = 8
VMEM_LIMIT = 16 * 1024 * 1024
TOKEN = (8, 128)

step_tau = 0.28
step_sigma = 0.28
radius = 0.3
rate = 0.5

keep_old = 1.0 / (1.0 + step_tau)
take_new = step_tau / (1.0 + step_tau)

PAIRS_X = [(0, 1), (1, 0), (2, 3), (3, 2)]
PAIRS_Y = [(0, 2), (2, 0), (1, 3), (3, 1)]
PAIRS_FAR = [(0, 3), (3, 0), (1, 2), (2, 1)]


def near_core(arrays):
    return [pltpu.with_memory_space_constraint(array, pltpu.VMEM) for array in arrays]


def swap_x(array):
    return lax.ppermute(array, "shot", PAIRS_X)


def swap_y(array):
    return lax.ppermute(array, "shot", PAIRS_Y)


def swap_far(array):
    return lax.ppermute(array, "shot", PAIRS_FAR)


def params():
    return pltpu.CompilerParams(vmem_limit_bytes=VMEM_LIMIT)


COST = pl.CostEstimate(flops=1, bytes_accessed=1, transcendentals=0)
HUGE = pl.CostEstimate(flops=1, bytes_accessed=1_000_000_000, transcendentals=0)
LONG = pl.CostEstimate(flops=1, bytes_accessed=100_000_000, transcendentals=0)


def tile_rows(rows):
    return slice(rows * SIDE, rows * SIDE + SIDE)


def gray(place):
    return place ^ (place >> 1)


def whereabouts(planes, rows, shares, paired):
    at = gray(lax.axis_index("shot"))
    layer = lax.axis_index("depth")
    flip = (1 - layer) if paired else 0 * layer
    start_x = lax.axis_index("inline") * rows + at * (rows // shares)
    return (at, at ^ 1, at ^ 2, at ^ 3, flip, layer * planes, start_x)


WHOLE = pl.BlockSpec(memory_space=pltpu.VMEM)
SCALARS = pl.BlockSpec(memory_space=pltpu.SMEM)
ANYWHERE = pl.BlockSpec(memory_space=pl.ANY)
FLIP, START_Z, START_X = (4, 5, 6)


def turn(flip, offset, count, total):
    return jnp.where(flip == 1, total - offset - count, offset)


def factor(signs):
    return (2 * signs[...] - 1).astype(jnp.float32)


def share_rows(spot, which, share):
    return pl.ds(pl.multiple_of(spot[which] * share, share), share)


def chunk_planes(spot, chunk, planes):
    offset, count = chunk
    return pl.ds(turn(spot[FLIP], offset, count, planes), count)


def fetch(source, spot, chunk, which, side, into, sem):
    planes, share, width = (source.shape[-3], into.shape[-2], into.shape[-1])
    place = (chunk_planes(spot, chunk, planes), share_rows(spot, which, share), pl.ds(side, width))
    if len(source.shape) == 4:
        place = (0,) + place
    copy = pltpu.make_async_copy(source.at[place], into, sem)
    copy.start()
    return copy


def prepare_kernel(chunk, after, spot, signs, gradient, *rest):
    spot = whereabouts(*spot)
    out_a, out_b, token, held, held_signs, sems = rest[after:]
    token[...] = jnp.zeros(token.shape, jnp.float32)
    half = out_a.shape[3]
    copy_signs = pltpu.make_async_copy(signs, held_signs, sems.at[4])
    copy_signs.start()
    todo = [(out_a, i, which, 0) for i, which in enumerate((1, 2))]
    todo += [(out_b, i, which, half) for i, which in enumerate((3, 2))]
    copies = [fetch(gradient, spot, chunk, which, side, held.at[n], sems.at[n]) for n, (_, _, which, side) in enumerate(todo)]
    copy_signs.wait()
    sign = factor(held_signs)[None]
    for n, (out, i, _, side) in enumerate(todo):
        copies[n].wait()
        out[i] = held[n] * sign[:, :, side : side + half]


def prepare(chunk, spot, signs, gradient, shares, after=(), keep=False):
    rows, cols = gradient.shape[2:]
    shape = (2, chunk[1], rows // shares, cols // 2)
    return pl.pallas_call(
        functools.partial(prepare_kernel, chunk, len(after), spot),
        in_specs=[ANYWHERE] * 2 + [WHOLE] * len(after),
        out_specs=[WHOLE] * 3,
        out_shape=[pltpu.VMEM(shape, jnp.float32) if keep else jax.ShapeDtypeStruct(shape, jnp.float32)] * 2
        + [jax.ShapeDtypeStruct(TOKEN, jnp.float32)],
        scratch_shapes=[
            pltpu.VMEM((4,) + shape[1:], jnp.float32),
            pltpu.VMEM(signs.shape, jnp.int32),
            pltpu.SemaphoreType.DMA((5,)),
        ],
        compiler_params=params(),
        cost_estimate=COST,
    )(signs, gradient, *near_core(after))


def hold_kernel(chunks, after, spot, signs, gradient, model, *rest):
    spot = whereabouts(*spot)
    fore_a, fore_b, base, held_a, held_b, held, held_signs, sems = rest[after:]
    half = fore_a.shape[2]
    copy_signs = pltpu.make_async_copy(signs, held_signs, sems.at[4 * len(chunks)])
    copy_signs.start()
    todo = []
    for chunk in chunks:
        here = pl.ds(*chunk)
        parts = ((gradient, 3, 0, held_a), (gradient, 1, half, held_b), (gradient, 0, 0, held.at[0]), (model, 0, 0, held.at[1]))
        copies = [
            fetch(source, spot, chunk, which, side, into.at[here], sems.at[len(todo) * 4 + n])
            for n, (source, which, side, into) in enumerate(parts)
        ]
        todo.append((copies, slice(chunk[0], chunk[0] + chunk[1])))
    copy_signs.wait()
    sign = factor(held_signs)[None]
    for copies, here in todo:
        for copy in copies:
            copy.wait()
        fore_a[here] = held_a[here] * sign[:, :, :half]
        fore_b[here] = held_b[here] * sign[:, :, half:]
        base[here] = held[1, here] - rate * (held[0, here] * sign)


def hold(chunks, spot, signs, gradient, model, shares, after=()):
    planes, rows, cols = model.shape
    whole = (planes, rows // shares, cols)
    part = (planes, rows // shares, cols // 2)
    return pl.pallas_call(
        functools.partial(hold_kernel, chunks, len(after), spot),
        in_specs=[ANYWHERE] * 3 + [WHOLE] * len(after),
        out_specs=[WHOLE] * 3,
        out_shape=[pltpu.VMEM(shape, jnp.float32) for shape in (part, part, whole)],
        scratch_shapes=[
            pltpu.VMEM(part, jnp.float32),
            pltpu.VMEM(part, jnp.float32),
            pltpu.VMEM((2,) + whole, jnp.float32),
            pltpu.VMEM(signs.shape, jnp.int32),
            pltpu.SemaphoreType.DMA((4 * len(chunks) + 1,)),
        ],
        compiler_params=params(),
        cost_estimate=COST,
    )(signs, gradient, model, *near_core(after))


def relay_kernel(chunk, carried, ready, after, fore_a, fore_b, near_a, near_b, *rest):
    outs = rest[carried + ready + after :]
    here = slice(chunk[0], chunk[0] + chunk[1])
    at = 0
    if ready:
        at = rest[carried].shape[0]
        outs[0][:at] = rest[carried][...]
        outs[1][:at] = rest[carried + 1][...]
    outs[0][at:] = fore_a[here] + near_a[1]
    outs[1][at:] = fore_b[here] + near_b[1]
    for source, out in zip(rest[:carried], outs[2:]):
        out[...] = source[...]
    outs[-1][...] = jnp.zeros(outs[-1].shape, jnp.float32)


def relay(chunk, fores, near, carried=(), after=(), ready=()):
    count = chunk[1] + sum(array.shape[0] for array in ready[:1])
    shapes = [(count,) + near[0].shape[2:]] * 2 + [array.shape for array in carried] + [TOKEN]
    outs = pl.pallas_call(
        functools.partial(relay_kernel, chunk, len(carried), len(ready), len(after)),
        in_specs=[WHOLE] * (4 + len(carried) + len(ready) + len(after)),
        out_specs=[WHOLE] * len(shapes),
        out_shape=[jax.ShapeDtypeStruct(shape, jnp.float32) for shape in shapes],
        compiler_params=params(),
        cost_estimate=COST,
    )(*fores, *near_core((*near, *carried, *ready, *after)))
    return outs[:2], outs[2:-1], outs[-1]


def settle_kernel(chunks, edges, after, spot, base, *refs):
    spot = whereabouts(*spot)
    nears, (far_a, far_b) = (refs[: 2 * len(chunks)], refs[2 * len(chunks) : 2 * len(chunks) + 2])
    out, *sides = refs[2 * len(chunks) + 2 + after :]
    half = far_a.shape[2]
    at = 0
    for k, (start, count) in enumerate(chunks):
        here = slice(at, at + count)
        for side, near, far in ((slice(0, half), nears[2 * k], far_a), (slice(half, 2 * half), nears[2 * k + 1], far_b)):
            out[here, :, side] = base[start : start + count, :, side] - rate * (near[0] + far[here])
        at += count
    if edges:
        odd = spot[0] % 2 == 1
        for p in range(out.shape[0]):
            last = out[p, out.shape[1] - HALO :]
            first = out[p, :HALO]
            sides[0][p] = jnp.where(odd, first, last)
            sides[1][p] = jnp.where(odd, last, first)


def settle(chunks, spot, base, nears, fars, after=(), edges=False):
    count, share, half = fars[0].shape
    shapes = [(count, share, 2 * half)] + ([(count, HALO, 2 * half)] * 2 if edges else [])
    return pl.pallas_call(
        functools.partial(settle_kernel, chunks, edges, len(after), spot),
        in_specs=[WHOLE] * (3 + len(nears) + len(after)),
        out_specs=[WHOLE] * len(shapes),
        out_shape=[jax.ShapeDtypeStruct(shape, jnp.float32) for shape in shapes],
        compiler_params=params(),
        cost_estimate=COST,
    )(base, *near_core((*nears, *fars, *after)))


def pack_kernel(count, spot, *refs):
    spot = whereabouts(*spot)
    parts, (one, two) = (refs[:count], refs[count:])
    odd = spot[0] % 2 == 1
    at = 0
    for part in parts:
        for p in range(part.shape[0]):
            last = part[p, part.shape[1] - HALO :]
            first = part[p, :HALO]
            one[at] = jnp.where(odd, first, last)
            two[at] = jnp.where(odd, last, first)
            at += 1


def pack(spot, parts):
    shape = (sum(part.shape[0] for part in parts), HALO, parts[0].shape[2])
    return pl.pallas_call(
        functools.partial(pack_kernel, len(parts), spot),
        in_specs=[WHOLE] * len(parts),
        out_specs=[WHOLE] * 2,
        out_shape=[jax.ShapeDtypeStruct(shape, jnp.float32)] * 2,
        compiler_params=params(),
        cost_estimate=COST,
    )(*near_core(parts))


def vary_kernel(span, pieces, sizes, counts, after, spot, *refs):
    spot = whereabouts(*spot)
    fields, befores, afters = (refs[: counts[0]], refs[counts[0] : counts[0] + counts[1]], refs[counts[0] + counts[1] : counts[0] + 2 * counts[1]])
    out, target, primal, ahead, dual = refs[counts[0] + 2 * counts[1] + after :]
    planes, rows, cols = target.shape
    depth_planes, total_z, total_x = sizes
    share = rows - SIDE
    half = cols // 2
    tiles = share // SIDE
    shape = (SIDE, cols)
    flip = spot[FLIP]
    odd = spot[0] % 2 == 1

    for field, held, offset, count, side, line, there, base in pieces:
        goes = turn(flip, there, count, planes)
        if field is None:
            for i in range(count):
                target[goes + i] = jnp.zeros((rows, cols), jnp.float32)
            continue
        comes = turn(flip, offset, count, held)
        for i in range(count):
            target[goes + i, :share] = fields[field][base + comes + i]
            target[goes + i, share:rows] = jnp.zeros(shape, jnp.float32)
            one = befores[side][line + comes + i]
            two = afters[side][line + comes + i]
            target[goes + i, share : share + HALO] = jnp.where(odd, two, one)
            target[goes + i, rows - HALO : rows] = jnp.where(odd, one, two)

    row = lax.broadcasted_iota(jnp.int32, shape, 0)
    col = lax.broadcasted_iota(jnp.int32, shape, 1)
    first_row, last_row = (row == 0, row == SIDE - 1)
    coef_y = jnp.where(col < cols - 1, jnp.float32(step_sigma), jnp.float32(0))
    start_x = spot[START_X]
    start_z = spot[START_Z] + turn(flip, span[0] - HALO, planes, depth_planes)

    def coef_x(place):
        return jnp.where((place >= 0) & (place <= total_x - 2), jnp.float32(step_sigma), jnp.float32(0))

    edge_x = {
        tiles - 1: coef_x(start_x + share - SIDE + row),
        tiles: coef_x(start_x + jnp.where(row < SIDE // 2, share + row, row - SIDE)),
    }

    for step in range(ITERS):
        source = target if step == 0 else ahead
        old = target if step == 0 else primal

        def plane(p, carry):
            place = start_z + p
            coef_z = jnp.where((place >= 0) & (place <= total_z - 2), jnp.float32(step_sigma), jnp.float32(0))
            rows_of = [tile_rows(t) for t in range(tiles + 1)]
            tile = [source[p, here] for here in rows_of]
            below = [source[p + 1, here] for here in rows_of]
            before_z = [dual[0, max(p - 1, 0), here] for here in rows_of]
            if step > 0:
                olds = [[dual[i, p, here] for here in rows_of] for i in range(3)]
                old_value = [old[p, here] for here in rows_of]
                goal = [target[p, here] for here in rows_of]
            else:
                old_value, goal = (tile, tile)
            turned = [pltpu.roll(v, SIDE - 1, 0) for v in tile]
            aside = [pltpu.roll(v, cols - 1, 1) for v in tile]
            all_steps = []
            for t in range(tiles + 1):
                v = tile[t]
                beyond = turned[(t + 1) % (tiles + 1)]
                step_z = coef_z * (below[t] - v)
                step_x = edge_x.get(t, jnp.float32(step_sigma)) * (jnp.where(last_row, beyond, turned[t]) - v)
                step_y = coef_y * (aside[t] - v)
                if step > 0:
                    step_z = step_z + olds[0][t]
                    step_x = step_x + olds[1][t]
                    step_y = step_y + olds[2][t]
                square = step_z * step_z + step_x * step_x + step_y * step_y
                scale = jnp.minimum(jnp.float32(1), jnp.float32(radius) * lax.rsqrt(square))
                all_steps.append((step_z * scale, step_x * scale, step_y * scale))
            moved = [pltpu.roll(steps[1], 1, 0) for steps in all_steps]
            aside = [pltpu.roll(steps[2], 1, 1) for steps in all_steps]
            news = []
            needed = 0 if p == step else tiles + 1 if step < ITERS - 1 else tiles
            for t in range(needed):
                step_z, step_x, step_y = all_steps[t]
                last_x = moved[t - 1 if t else tiles]
                diverge = (step_z - before_z[t]) + (step_x - jnp.where(first_row, last_x, moved[t])) + (step_y - aside[t])
                news.append(jnp.float32(keep_old) * old_value[t] + jnp.float32(take_new) * (diverge + goal[t]))
            for t, here in enumerate(rows_of):
                dual[0, p, here] = all_steps[t][0]
                if p == step:
                    continue
                if step < ITERS - 1:
                    dual[1, p, here] = all_steps[t][1]
                    dual[2, p, here] = all_steps[t][2]
                    primal[p, here] = news[t]
                    ahead[p, here] = 2.0 * news[t] - old_value[t]
                elif t < tiles:
                    place_out = max(p - HALO, 0)
                    out[0, place_out, here] = news[t][:, :half]
                    out[1, place_out, here] = news[t][:, half:]
            return carry

        for p in range(step, planes - 1 - step):
            plane(p, 0)


def vary(span, pieces, sizes, spot, fields, befores, afters, after=()):
    _, share, cols = fields[0].shape
    planes, rows = (span[1] - span[0] + 2 * HALO, share + SIDE)
    field = pltpu.VMEM((planes, rows, cols), jnp.float32)
    counts = (len(fields), len(befores))
    return pl.pallas_call(
        functools.partial(vary_kernel, span, pieces, sizes, counts, len(after), spot),
        in_specs=[WHOLE] * (counts[0] + 2 * counts[1]) + [WHOLE] * len(after),
        out_specs=WHOLE,
        out_shape=jax.ShapeDtypeStruct((2, span[1] - span[0], share, cols // 2), jnp.float32),
        scratch_shapes=[field, field, field, pltpu.VMEM((3, planes, rows, cols), jnp.float32)],
        compiler_params=params(),
        cost_estimate=LONG,
    )(*near_core((*fields, *befores, *afters, *after)))


def gather_kernel(span, parts, spot, *refs):
    spot = whereabouts(*spot)
    out, sems = refs[-2:]
    layers = chunk_planes(spot, (span[0], span[1] - span[0]), out.shape[0])
    copies = []
    for ref, (which, sides) in zip(refs, parts):
        share, half = ref.shape[-2:]
        for n, side in enumerate(sides):
            there = out.at[layers, share_rows(spot, which, share), pl.ds(side * half, half)]
            source = ref.at[n] if len(ref.shape) == 4 else ref
            copies.append(pltpu.make_async_copy(source, there, sems.at[len(copies)]))
    for copy in copies:
        copy.start()
    for copy in copies:
        copy.wait()


def gather(span, spot, out_shape, pieces, so_far=None, cost=COST):
    before = [] if so_far is None else [so_far]
    arrays, parts = zip(*((array, (which, sides)) for array, which, sides in pieces))
    return pl.pallas_call(
        functools.partial(gather_kernel, span, parts, spot),
        in_specs=[ANYWHERE] * (len(arrays) + len(before)),
        out_specs=pl.BlockSpec(memory_space=pltpu.HBM),
        out_shape=jax.ShapeDtypeStruct(out_shape, jnp.float32),
        input_output_aliases={len(arrays): 0} if before else {},
        scratch_shapes=[pltpu.SemaphoreType.DMA((8,))],
        compiler_params=params(),
        cost_estimate=cost,
    )(*arrays, *before)


def carry_kernel(count, after, *refs):
    for source, out in zip(refs[:count], refs[count + after :]):
        out[...] = source[...]


def carry(arrays, after):
    return pl.pallas_call(
        functools.partial(carry_kernel, len(arrays), len(after)),
        in_specs=[WHOLE] * (len(arrays) + len(after)),
        out_specs=[WHOLE] * len(arrays),
        out_shape=[jax.ShapeDtypeStruct(array.shape, array.dtype) for array in arrays],
        compiler_params=params(),
        cost_estimate=COST,
    )(*near_core((*arrays, *after)))


def spread(own):
    from_x, from_y = (swap_x(own), swap_y(own))
    far_a, far_b = (swap_x(from_y[0]), swap_y(from_x[1]))
    return ((own, 0, (0, 1)), (from_x, 1, (0, 1)), (far_a, 2, (0,)), (far_b, 2, (1,)), (from_y, 3, (0, 1)))


def spread_halves(own):
    y_a, x_b = (swap_y(own[0]), swap_x(own[1]))
    x_a, y_b = (swap_x(own[0]), swap_y(own[1]))
    far_a, far_b = (swap_x(y_a), swap_y(x_b))
    return (
        (own, 0, (0, 1)), (x_a, 1, (0,)), (x_b, 1, (1,)), (far_a, 2, (0,)), (far_b, 2, (1,)), (y_a, 3, (0,)), (y_b, 3, (1,))
    )


def spread_at_once(own):
    return ((own, 0, (0, 1)), (swap_x(own), 1, (0, 1)), (swap_far(own), 2, (0, 1)), (swap_y(own), 3, (0, 1)))


def body(gradient, signs, model):
    shares, lines, layers = (lax.axis_size(name) for name in ("shot", "inline", "depth"))
    planes, rows, cols = model.shape
    share = rows // shares
    sizes = (planes, planes * layers, rows * lines)
    paired = layers == 2
    spot = (planes, rows, shares, paired)
    flip = whereabouts(*spot)[FLIP]

    order = [gray(place) * lines + line for line in range(lines) for place in range(shares)]
    pairs_one = [pair for i, j in zip(order[::2], order[1::2]) for pair in ((i, j), (j, i))]
    pairs_two = [pair for i, j in zip(order[1:-1:2], order[2::2]) for pair in ((i, j), (j, i))]
    ahead_z = [(i, i + 1) for i in range(layers - 1)]
    back_z = [(j, i) for i, j in ahead_z]

    def across(edges):
        group = ("shot", "inline")
        return [lax.ppermute(edge, group, pairs) for edge, pairs in zip(edges, (pairs_one, pairs_two))]

    gradient = pltpu.with_memory_space_constraint(gradient, pltpu.HBM)
    model = pltpu.with_memory_space_constraint(model, pltpu.HBM)
    signs = pltpu.with_memory_space_constraint(signs, pltpu.HBM)

    def both(a, b):
        return swap_x(a), swap_y(b)

    def crossed(a, b):
        return swap_y(a), swap_x(b)

    def prep(chunk, after=()):
        return prepare(chunk, spot, signs, gradient, shares, after)

    if not paired:
        c0 = (0, planes)
        *sent, token = prep(c0)
        near = both(*sent)
        *fores, base = hold([c0], spot, signs, gradient, model, shares, (token,))
        far = crossed(*relay(c0, fores, near)[0])
        (target,) = settle([c0], spot, base, near, far)
        low = lax.ppermute(target[planes - HALO :], "depth", ahead_z)
        high = lax.ppermute(target[:HALO], "depth", back_z)
        before, after = across(pack(spot, (low, target, high)))
        pieces = [
            (0, HALO, 0, HALO, 0, 0, 0, 0),
            (1, planes, 0, planes, 0, HALO, HALO, 0),
            (2, HALO, 0, HALO, 0, HALO + planes, HALO + planes, 0),
        ]
        own = vary((0, planes), pieces, sizes, spot, (low, target, high), (before,), (after,))
        return gather((0, planes), spot, model.shape, spread(own))

    n0, n1 = ((7 * planes) // 16, planes // 4)
    n2 = planes - n0 - n1
    c0, c1, c2 = ((0, n0), (n0, n1), (n0 + n1, n2))
    *sent_0, token_0 = prep(c0)
    near_0 = both(*sent_0)
    *sent_1, token_1 = prep(c1, (token_0,))
    near_1 = both(*sent_1)
    *fores, base = hold([c0, c1, c2], spot, signs, gradient, model, shares, (token_1,))
    *sent_2, token_2 = prepare(c2, spot, signs, gradient, shares, (base,), True)
    passed_0, _, token_3 = relay(c0, fores, near_0, after=(token_2,))
    far_0 = crossed(*passed_0)
    passed_1, sent_2, token_4 = relay(c1, fores, near_1, sent_2, (token_3,))
    near_2 = both(*sent_2)
    (mid_0,) = settle([c0], spot, base, near_0, far_0, (token_4,))
    edge = lax.dynamic_slice_in_dim(mid_0, turn(flip, 0, HALO, n0), HALO, 0)
    beside = lax.ppermute(edge, "depth", ahead_z + back_z)
    edges_0 = pack(spot, (mid_0, beside))
    before_0, after_0 = across(edges_0)
    passed_2, _, token_5 = relay(c2, fores, near_2, after=edges_0, ready=passed_1)
    far_1 = crossed(*passed_2)
    arrays = {"beside": beside, "mid_0": mid_0, }
    sides = [(before_0, after_0)]
    held = [
        (-HALO, HALO, "beside", 0, 0, n0),
        (0, n0, "mid_0", 0, 0, 0),
        (n0, n1, "mid_1", 0, 1, 0),
        (n0 + n1, n2, "mid_1", n1, 1, n1),
        (planes, HALO, None, 0, 0, 0),
    ]

    def update(span, after=()):
        start, stop = (span[0] - HALO, span[1] + HALO)
        names, used, pieces = ([], [], [])
        for first, count, name, base, side, line in held:
            low, high = (max(first, start), min(first + count, stop))
            if low >= high:
                continue
            if name is not None:
                names += [name] if name not in names else []
                used += [side] if side not in used else []
            pieces.append((name, first, count, base, side, line, low, high))
        plan = []
        for name, first, count, base, side, line, low, high in pieces:
            if name is None:
                plan.append((None, 0, 0, high - low, 0, 0, low - start, 0))
            else:
                plan.append((names.index(name), count, low - first, high - low, used.index(side), line, low - start, base))
        return vary(
            span, plan, sizes, spot, [arrays[n] for n in names], [sides[i][0] for i in used], [sides[i][1] for i in used], after
        )

    m0 = n0 - HALO
    m1 = (m0 + planes) // 2
    spans = ((0, m0), (m0, m1), (m1, planes))
    own_0 = update(spans[0], (token_5,))
    mid_1, *edges_1 = settle([c1, c2], spot, base, near_1 + near_2, far_1, (own_0,), True)
    before_1, after_1 = across(edges_1)
    arrays["mid_1"] = mid_1
    sides.append((before_1, after_1))
    pieces_0 = spread(own_0)
    own_1 = update(spans[1], (own_0,))
    pieces_1 = spread(own_1)
    own_2 = update(spans[2], (own_1, pieces_0[1][0], pieces_0[4][0]))
    out = gather(spans[0], spot, model.shape, pieces_0)
    out = gather(spans[1], spot, model.shape, pieces_1, out)
    out = gather(spans[2], spot, model.shape, spread_halves(own_2), out)
    return out


def solution(mesh):
    placed = (P("shot", "depth", "inline", None), P("shot", None), P("depth", "inline", None))
    return jax.shard_map(
        body, mesh=mesh, in_specs=placed, out_specs=P("depth", "inline", None), check_vma=False
    )
```
